32 devices in a mesh: seq: 16 (over z, x, core), head: 2 (over y).
Axes of the slice: x: 2, y: 2, z: 4, core: 2. Of those that a mesh axis runs over, the one named last changes fastest.
Arguments:
- queries: bfloat16 [8192, 4096], P(('seq', 'head'))
- key_vectors: bfloat16 [8192, 4096], P(('seq', 'head'))
- value_vectors: bfloat16 [8192, 4096], P(('seq', 'head')), may hold values from -6 to 6
- out_grads: bfloat16 [8192, 4096], P(('seq', 'head')), may hold values from -6 to 6
- extra_blocks: int32 [16, 8, 8], P('seq'), may hold values 0 or 1
- summary_rows: int32 [16, 16], P('seq'), may hold values from 0 to 511, as said below
Outputs:
- attention: bfloat16 [8192, 4096], P(('seq', 'head'))
- query_grad: bfloat16 [8192, 4096], P(('seq', 'head'))
- key_grad: bfloat16 [8192, 4096], P(('seq', 'head'))
- value_grad: bfloat16 [8192, 4096], P(('seq', 'head'))
The draws below stay inside these ranges and needn't reach their ends.
Inputs may be any that keep to these rules, and one draw needn't show every extreme that they name: `summary_rows`: summary row s of a group lies in [s * 32, (s + 1) * 32), so the rows of a group are distinct and ascending.
All inputs are finite; a program needn't handle non-finite values. No bound on the sum of `extra_blocks` on one device may be relied on, other than what follows from the above.
Results may differ from the reference program's by a relative error of at most 0.022.
Values may be sent and summed in bfloat16 or wider, within the bound.
No kernel may reach another device: no remote copies, remote signals or barrier semaphores. Data moves between devices by JAX's collectives and lax.ppermute only.
A program may use at most 128 MiB of HBM per device.

```python
import jax
import jax.numpy as jnp
from jax import lax

HEADS = 32
HD = 128
GROUP = 512
SUMM = 16
NBLK = 8
GROUPS = 16
TOKENS = 8192
FEAT = 4096


def paired_fields(key):
    base = jax.random.fold_in(key, 4099)
    key_query, key_keys = jax.random.split(base, 2)
    row_count = TOKENS
    query_draw = 2.5 * jnp.clip(jax.random.normal(key_query, (row_count, HEADS, HD)), -6.0, 6.0)
    key_draw = jnp.clip(jax.random.normal(key_keys, (row_count, HEADS, HD)), -6.0, 6.0)
    return (query_draw.reshape(row_count, FEAT), key_draw.reshape(row_count, FEAT))


def draw_queries(key, part):
    return paired_fields(key)[0].astype(jnp.bfloat16)


def draw_key_vectors(key, part):
    return paired_fields(key)[1].astype(jnp.bfloat16)


def draw_summary_rows(key, part):
    stride = GROUP // SUMM
    offsets = jax.random.randint(jax.random.fold_in(key, 11), (GROUPS, SUMM), 0, stride)
    offsets = offsets.at[0, 0].set(0).at[0, SUMM - 1].set(stride - 1)
    return (jnp.arange(SUMM)[None, :] * stride + offsets).astype(jnp.int32)


def plant(values, stream_key, low, top_value):
    index_at = [jax.random.randint(jax.random.fold_in(stream_key, axis), (), 0, length) for axis, length in enumerate(values.shape)]
    main_axis = values.shape.index(max(values.shape))
    beside = index_at[:main_axis] + [(index_at[main_axis] + 1) % values.shape[main_axis]] + index_at[main_axis + 1:]
    return values.at[tuple(index_at)].set(low).at[tuple(beside)].set(top_value)


def levels(key, extent, pieces, smallest, high):
    def one(dim, shards_of):
        draws = jax.random.uniform(jax.random.fold_in(jax.random.fold_in(key, 6), dim), (shards_of,), jnp.float32, smallest / len(pieces), high / len(pieces))
        return jnp.repeat(jnp.exp(draws), extent[dim] // shards_of).reshape((-1,) + (1,) * (len(extent) - dim - 1))

    gain = one(*pieces[0])
    for cut in pieces[1:]:
        gain = gain * one(*cut)
    return gain


def bell_draw(rng, dims, deviation, bound, cuts=(), kind=jnp.bfloat16):
    entries = deviation * jax.random.normal(rng, dims, jnp.float32)
    if cuts:
        entries = entries * levels(rng, dims, cuts, -0.22, 0.18)
    return jnp.clip(entries, -bound, bound).astype(kind)


def setup_inputs(seed: int = 0) -> dict:
    seeds = jax.random.split(jax.random.key(seed), 7)
    return {
        "queries": draw_queries(jax.random.fold_in(seeds[6], 71), 0),
        "key_vectors": draw_key_vectors(jax.random.fold_in(seeds[6], 71), 0),
        "value_vectors": bell_draw(seeds[2], (TOKENS, FEAT), 1.0, 6.0, ((0, 32),)),
        "out_grads": bell_draw(seeds[3], (TOKENS, FEAT), 1.0, 6.0, ((0, 32),)),
        "extra_blocks": plant((jax.random.randint(seeds[4], (GROUPS, NBLK, NBLK), 0, 3) < 1).astype(jnp.int32), jax.random.fold_in(seeds[4], 1), 0, 1),
        "summary_rows": draw_summary_rows(jax.random.fold_in(seeds[6], 71), 0),
    }


neg_big = -1.0e30


def local_allowed(extra_map, group_len):
    block_count = extra_map.shape[0]
    block_len = group_len // block_count
    block_ids = jnp.arange(block_count, dtype=jnp.int32)
    block_lag = block_ids[:, None] - block_ids[None, :]
    allowed = (block_lag == 0) | (block_lag == 1) | ((extra_map == 1) & (block_lag > 0))
    allowed = jnp.repeat(jnp.repeat(allowed, block_len, axis=0), block_len, axis=1)
    positions = jnp.arange(group_len, dtype=jnp.int32)
    return allowed & (positions[None, :] <= positions[:, None])


def reference(queries, key_vectors, value_vectors, out_grads, extra_blocks, summary_rows):
    factor = HD ** -0.5
    query_heads = queries.reshape(GROUPS, GROUP, HEADS, HD)
    key_heads = key_vectors.reshape(GROUPS, GROUP, HEADS, HD)
    val_heads = value_vectors.reshape(GROUPS, GROUP, HEADS, HD)
    grad_heads = out_grads.reshape(GROUPS, GROUP, HEADS, HD)
    positions = (jnp.arange(GROUPS, dtype=jnp.int32)[:, None] * GROUP + summary_rows.astype(jnp.int32)).reshape(-1)
    summary_keys = key_vectors.reshape(TOKENS, HEADS, HD)[positions].astype(jnp.float32)
    summary_vals = value_vectors.reshape(TOKENS, HEADS, HD)[positions].astype(jnp.float32)
    owners = jnp.arange(GROUPS * SUMM, dtype=jnp.int32) // SUMM

    def advance(carried, inputs):
        key_sums, val_sums = carried
        query_c, key_c, val_c, grad_c, extra_map, rows_c, group_id = inputs
        allowed = jnp.concatenate([local_allowed(extra_map, GROUP), jnp.broadcast_to(owners[None, :] < group_id, (GROUP, GROUPS * SUMM))], axis=1)
        all_keys = jnp.concatenate([key_c.astype(jnp.float32), summary_keys], axis=0)
        all_vals = jnp.concatenate([val_c.astype(jnp.float32), summary_vals], axis=0)
        query_f = query_c.astype(jnp.float32)
        grad_f = grad_c.astype(jnp.float32)
        scores = jnp.where(allowed[None], jnp.einsum("qhd,khd->hqk", query_f, all_keys) * factor, neg_big)
        peak = jnp.max(scores, axis=2, keepdims=True)
        log_mass = jnp.log(jnp.sum(jnp.exp(scores - peak), axis=2, keepdims=True)) + peak
        attn_probs = jnp.where(allowed[None], jnp.exp(scores - log_mass), 0.0)
        weights = lax.optimization_barrier(attn_probs.astype(jnp.bfloat16)).astype(jnp.float32)
        attention = jnp.einsum("hqk,khd->qhd", weights, all_vals).astype(jnp.bfloat16)
        row_dot = jnp.einsum("qhd,qhd->hq", grad_f, attention.astype(jnp.float32))
        prob_grads = jnp.einsum("qhd,khd->hqk", grad_f, all_vals)
        score_grads = lax.optimization_barrier((attn_probs * (prob_grads - row_dot[..., None])).astype(jnp.bfloat16)).astype(jnp.float32)
        query_grad = (jnp.einsum("hqk,khd->qhd", score_grads, all_keys) * factor).astype(jnp.bfloat16)
        key_part = jnp.einsum("hqk,qhd->khd", score_grads, query_f) * factor
        val_part = jnp.einsum("hqk,qhd->khd", weights, grad_f)
        key_sums = key_sums + key_part[GROUP:]
        val_sums = val_sums + val_part[GROUP:]
        own_keys = lax.dynamic_slice_in_dim(key_sums, group_id * SUMM, SUMM, 0)
        own_vals = lax.dynamic_slice_in_dim(val_sums, group_id * SUMM, SUMM, 0)
        key_grad = key_part[:GROUP].at[rows_c].add(own_keys).astype(jnp.bfloat16)
        value_grad = val_part[:GROUP].at[rows_c].add(own_vals).astype(jnp.bfloat16)
        return (key_sums, val_sums), (attention, query_grad, key_grad, value_grad)

    start_sums = (jnp.zeros((GROUPS * SUMM, HEADS, HD), jnp.float32), jnp.zeros((GROUPS * SUMM, HEADS, HD), jnp.float32))
    inputs = (query_heads, key_heads, val_heads, grad_heads, extra_blocks, summary_rows.astype(jnp.int32), jnp.arange(GROUPS, dtype=jnp.int32))
    finals, stacked = lax.scan(advance, start_sums, inputs, reverse=True)
    attention, query_grad, key_grad, value_grad = stacked
    return (attention.reshape(TOKENS, FEAT), query_grad.reshape(TOKENS, FEAT), key_grad.reshape(TOKENS, FEAT), value_grad.reshape(TOKENS, FEAT))
```

```python
import functools
import math

import jax
import jax.numpy as jnp
from jax import lax
from jax.experimental import pallas as pl
from jax.experimental.pallas import tpu as pltpu
from jax.sharding import PartitionSpec as P

HD = 128


neg_big = -1e30
pos_big = 3e38


def head_scores(query_heads, key_heads, factor):
    return (
        jnp.einsum("qhd,khd->hqk", query_heads, key_heads, preferred_element_type=jnp.float32)
        * factor
    )


def local_allowed(extra_map, group_len):
    block_count = extra_map.shape[0]
    block_len = group_len // block_count
    block_ids = jnp.arange(block_count, dtype=jnp.int32)
    block_lag = block_ids[:, None] - block_ids[None, :]
    allowed = (block_lag == 0) | (block_lag == 1) | (extra_map == 1) & (block_lag > 0)
    allowed = jnp.repeat(jnp.repeat(allowed, block_len, axis=0), block_len, axis=1)
    positions = jnp.arange(group_len, dtype=jnp.int32)
    return allowed & (positions[None, :] <= positions[:, None])


def key_window(summary_keys, summary_vals, block_id, key_rows, lower_end, upper_end, per_group):
    offset = block_id * key_rows
    key_block = lax.dynamic_slice_in_dim(summary_keys, offset, key_rows, 0)
    val_block = lax.dynamic_slice_in_dim(summary_vals, offset, key_rows, 0)
    owners = (offset + jnp.arange(key_rows, dtype=jnp.int32)) // per_group
    usable = (owners >= lower_end) & (owners < upper_end)
    return (offset, key_block, val_block, usable[None, None, :])


def block_bounds(lower_end, upper_end, key_rows, per_group):
    begin_block = lower_end * per_group // key_rows
    end_block = (upper_end * per_group + key_rows - 1) // key_rows
    return (begin_block, jnp.where(upper_end > lower_end, end_block, begin_block))


def softmax_stats(
    query_heads, summary_keys, summary_vals, lower_end, upper_end, key_rows, per_group, factor
):
    begin_block, end_block = block_bounds(lower_end, upper_end, key_rows, per_group)

    def softmax_advance(block_id, carried):
        peak, summed = carried
        offset, key_block, val_block, usable = key_window(
            summary_keys, summary_vals, block_id, key_rows, lower_end, upper_end, per_group
        )
        scores = jnp.where(usable, head_scores(query_heads, key_block, factor), neg_big)
        new_peak = jnp.maximum(peak, jnp.max(scores, axis=2))
        summed = summed * jnp.exp(peak - new_peak) + jnp.sum(
            jnp.exp(scores - new_peak[..., None]), axis=2
        )
        return (new_peak, summed)

    shape_hq = (query_heads.shape[1], query_heads.shape[0])
    start_stats = (jnp.full(shape_hq, neg_big, jnp.float32), jnp.zeros(shape_hq, jnp.float32))
    return lax.fori_loop(begin_block, end_block, softmax_advance, start_stats)


def merge_stats(earlier, later):
    peak = jnp.maximum(earlier[0], later[0])
    return (peak, earlier[1] * jnp.exp(earlier[0] - peak) + later[1] * jnp.exp(later[0] - peak))


def weighted_values(
    query_heads,
    log_mass,
    summary_keys,
    summary_vals,
    lower_end,
    upper_end,
    key_rows,
    per_group,
    factor,
):
    begin_block, end_block = block_bounds(lower_end, upper_end, key_rows, per_group)

    def weighted_advance(block_id, summed_values):
        offset, key_block, val_block, usable = key_window(
            summary_keys, summary_vals, block_id, key_rows, lower_end, upper_end, per_group
        )
        weights = jnp.where(
            usable, jnp.exp(head_scores(query_heads, key_block, factor) - log_mass[..., None]), 0.0
        ).astype(jnp.bfloat16)
        return summed_values + jnp.einsum(
            "hqk,khd->qhd", weights, val_block, preferred_element_type=jnp.float32
        )

    return lax.fori_loop(
        begin_block, end_block, weighted_advance, jnp.zeros(query_heads.shape, jnp.float32)
    )


def summary_backward(
    query_heads,
    grad_heads,
    log_mass,
    row_dot,
    summary_keys,
    summary_vals,
    lower_end,
    upper_end,
    key_rows,
    per_group,
    factor,
    carried,
):
    begin_block, end_block = block_bounds(lower_end, upper_end, key_rows, per_group)

    def summary_advance(block_id, running):
        query_acc, key_terms, val_terms = running
        offset, key_block, val_block, usable = key_window(
            summary_keys, summary_vals, block_id, key_rows, lower_end, upper_end, per_group
        )
        attn_probs = jnp.where(
            usable, jnp.exp(head_scores(query_heads, key_block, factor) - log_mass[..., None]), 0.0
        )
        weights = attn_probs.astype(jnp.bfloat16)
        prob_grads = jnp.einsum(
            "qhd,khd->hqk", grad_heads, val_block, preferred_element_type=jnp.float32
        )
        score_grads = (attn_probs * (prob_grads - row_dot[..., None])).astype(jnp.bfloat16)
        query_acc = (
            query_acc
            + jnp.einsum("hqk,khd->qhd", score_grads, key_block, preferred_element_type=jnp.float32)
            * factor
        )
        key_part = (
            jnp.einsum("hqk,qhd->khd", score_grads, query_heads, preferred_element_type=jnp.float32)
            * factor
        )
        val_part = jnp.einsum(
            "hqk,qhd->khd", weights, grad_heads, preferred_element_type=jnp.float32
        )
        key_terms = lax.dynamic_update_slice_in_dim(
            key_terms,
            lax.dynamic_slice_in_dim(key_terms, offset, key_rows, 0) + key_part,
            offset,
            0,
        )
        val_terms = lax.dynamic_update_slice_in_dim(
            val_terms,
            lax.dynamic_slice_in_dim(val_terms, offset, key_rows, 0) + val_part,
            offset,
            0,
        )
        return (query_acc, key_terms, val_terms)

    return lax.fori_loop(begin_block, end_block, summary_advance, carried)


def per_device(queries, key_vectors, value_vectors, out_grads, extra_blocks, summary_rows):
    query_all, key_all, val_all, grad_all = (
        lax.all_to_all(queries, "head", split_axis=1, concat_axis=0, tiled=True),
        lax.all_to_all(key_vectors, "head", split_axis=1, concat_axis=0, tiled=True),
        lax.all_to_all(value_vectors, "head", split_axis=1, concat_axis=0, tiled=True),
        lax.all_to_all(out_grads, "head", split_axis=1, concat_axis=0, tiled=True),
    )
    group_len, local_width = query_all.shape
    head_count = local_width // HD
    factor = HD ** (-0.5)
    query_heads = query_all.reshape(group_len, head_count, HD)
    key_heads = key_all.reshape(group_len, head_count, HD)
    val_heads = val_all.reshape(group_len, head_count, HD)
    grad_heads = grad_all.reshape(group_len, head_count, HD)
    per_group = summary_rows.shape[1]
    seq_count = lax.axis_size("seq")
    group_id = lax.axis_index("seq")
    picker = summary_rows[0][:, None] == jnp.arange(group_len, dtype=jnp.int32)[None, :]
    own_keys = jnp.dot(
        picker.astype(jnp.bfloat16), key_all, preferred_element_type=jnp.float32
    ).astype(jnp.bfloat16)
    own_vals = jnp.dot(
        picker.astype(jnp.bfloat16), val_all, preferred_element_type=jnp.float32
    ).astype(jnp.bfloat16)
    summ_keys_flat, summ_vals_flat = (
        lax.all_gather(own_keys, "seq", axis=0, tiled=True),
        lax.all_gather(own_vals, "seq", axis=0, tiled=True),
    )
    total_rows = summ_keys_flat.shape[0]
    summary_keys = summ_keys_flat.reshape(total_rows, head_count, HD)
    summary_vals = summ_vals_flat.reshape(total_rows, head_count, HD)
    key_rows = per_group * math.gcd(seq_count, max(1, 128 // per_group))
    allowed = local_allowed(extra_blocks[0], group_len)
    local_scores = jnp.where(allowed[None], head_scores(query_heads, key_heads, factor), neg_big)
    local_peak = jnp.max(local_scores, axis=2)
    local_stats = (local_peak, jnp.sum(jnp.exp(local_scores - local_peak[..., None]), axis=2))
    all_stats = merge_stats(
        local_stats,
        softmax_stats(
            query_heads, summary_keys, summary_vals, 0, group_id, key_rows, per_group, factor
        ),
    )
    log_mass = all_stats[0] + jnp.log(all_stats[1])
    summ_values = weighted_values(
        query_heads, log_mass, summary_keys, summary_vals, 0, group_id, key_rows, per_group, factor
    )
    local_probs = jnp.exp(local_scores - log_mass[..., None])
    local_weights = local_probs.astype(jnp.bfloat16)
    attention = (
        summ_values
        + jnp.einsum("hqk,khd->qhd", local_weights, val_heads, preferred_element_type=jnp.float32)
    ).astype(jnp.bfloat16)
    row_dot = jnp.einsum("qhd,qhd->hq", grad_heads, attention, preferred_element_type=jnp.float32)
    local_prob_grads = jnp.einsum(
        "qhd,khd->hqk", grad_heads, val_heads, preferred_element_type=jnp.float32
    )
    local_score_grads = (local_probs * (local_prob_grads - row_dot[..., None])).astype(jnp.bfloat16)
    query_local = (
        jnp.einsum("hqk,khd->qhd", local_score_grads, key_heads, preferred_element_type=jnp.float32)
        * factor
    )
    key_local = (
        jnp.einsum(
            "hqk,qhd->khd", local_score_grads, query_heads, preferred_element_type=jnp.float32
        )
        * factor
    )
    val_local = jnp.einsum(
        "hqk,qhd->khd", local_weights, grad_heads, preferred_element_type=jnp.float32
    )
    empty_terms = jnp.zeros((total_rows, head_count, HD), jnp.float32)
    start_running = (jnp.zeros(query_heads.shape, jnp.float32), empty_terms, empty_terms)
    query_summ, key_terms, val_terms = summary_backward(
        query_heads,
        grad_heads,
        log_mass,
        row_dot,
        summary_keys,
        summary_vals,
        0,
        group_id,
        key_rows,
        per_group,
        factor,
        start_running,
    )
    recv_keys, recv_vals = (
        lax.all_to_all(
            key_terms.astype(jnp.bfloat16), "seq", split_axis=0, concat_axis=0, tiled=True
        ).astype(key_terms.dtype),
        lax.all_to_all(
            val_terms.astype(jnp.bfloat16), "seq", split_axis=0, concat_axis=0, tiled=True
        ).astype(val_terms.dtype),
    )
    summ_key_grad = jnp.sum(recv_keys.reshape(seq_count, per_group, head_count, HD), axis=0)
    summ_val_grad = jnp.sum(recv_vals.reshape(seq_count, per_group, head_count, HD), axis=0)
    picker_f = picker.astype(jnp.float32)
    key_grad = key_local + jnp.einsum(
        "sq,shd->qhd", picker_f, summ_key_grad, precision=lax.Precision.HIGHEST
    )
    value_grad = val_local + jnp.einsum(
        "sq,shd->qhd", picker_f, summ_val_grad, precision=lax.Precision.HIGHEST
    )
    query_grad = query_local + query_summ
    outputs = (
        attention.reshape(group_len, local_width),
        query_grad.astype(jnp.bfloat16).reshape(group_len, local_width),
        key_grad.astype(jnp.bfloat16).reshape(group_len, local_width),
        value_grad.astype(jnp.bfloat16).reshape(group_len, local_width),
    )
    attention_out, query_out, key_out, value_out = (
        lax.all_to_all(outputs[0], "head", split_axis=0, concat_axis=1, tiled=True),
        lax.all_to_all(outputs[1], "head", split_axis=0, concat_axis=1, tiled=True),
        lax.all_to_all(outputs[2], "head", split_axis=0, concat_axis=1, tiled=True),
        lax.all_to_all(outputs[3], "head", split_axis=0, concat_axis=1, tiled=True),
    )
    return (attention_out, query_out, key_out, value_out)


VMEM_GRANT = 60 * 1024 * 1024


def score_caps(extra_map, rows_here, half, group_id, stages, per_group):
    block_count = extra_map.shape[0]
    block_len = rows_here * 2 // block_count
    mine = block_count // 2
    blocks = jnp.arange(mine, dtype=jnp.int32)
    query_blocks = half * mine + blocks
    extra_here = lax.dynamic_slice_in_dim(extra_map, half * mine, mine, 0)

    def expand(first_key_block):
        lag = query_blocks[None, :] - (first_key_block + blocks)[:, None]
        extra_part = lax.dynamic_slice_in_dim(extra_here, first_key_block, mine, 1).T
        allowed = (lag == 0) | (lag == 1) | ((extra_part == 1) & (lag > 0))
        wide = jnp.broadcast_to(allowed[:, None, :, None], (mine, block_len, mine, block_len))
        return wide.reshape(rows_here, rows_here)

    positions = jnp.arange(rows_here, dtype=jnp.int32)
    own = expand(half * mine) & (positions[:, None] <= positions[None, :])
    lower = expand(0) & (half == 1)
    core = group_id % 2
    side = (group_id // 2) % 2
    level = group_id // 4
    d_core = jnp.arange(2, dtype=jnp.int32)[:, None, None]
    d_side = jnp.arange(2, dtype=jnp.int32)[None, :, None]
    from_level = level - jnp.arange(stages, dtype=jnp.int32)[None, None, :]
    owner = from_level * 4 + (side + d_side) % 2 * 2 + (core + d_core) % 2
    usable = jnp.repeat(((from_level >= 0) & (owner < group_id)).reshape(-1), per_group)
    summ = jnp.broadcast_to(usable[:, None], (usable.shape[0], rows_here))
    return jnp.where(jnp.concatenate([own, lower, summ], axis=0), pos_big, neg_big)


def attention_step(
    caps_ref,
    query_ref,
    key_ref,
    val_ref,
    grad_ref,
    lower_ref,
    near_ref,
    side_ref,
    core_ref,
    far_ref,
    *rest,
):
    attn_ref, query_grad_ref, local_ref, back_ref, near_grad_ref, far_grad_ref = rest[-6:]
    rows_here, width = query_ref.shape
    slots, _, per_group, _ = near_ref.shape
    part_rows = slots * per_group
    half_rows = 2 * part_rows
    factor = HD ** (-0.5)
    parts = range(width // HD)
    queries, grads, keys, vals, raws, prob_grads = [], [], [], [], [], []
    for part in parts:
        cols = slice(part * HD, (part + 1) * HD)
        queries.append(query_ref[:, cols])
        grads.append(grad_ref[:, cols])
        for kind, (own_ref, into) in enumerate(((key_ref, keys), (val_ref, vals))):
            into.append(
                jnp.concatenate(
                    [
                        own_ref[:, cols],
                        lower_ref[kind, :, cols],
                        near_ref[:, kind, :, cols].reshape(part_rows, HD),
                        side_ref[:, kind, :, cols].reshape(part_rows, HD),
                        core_ref[:, kind, :, cols].reshape(part_rows, HD),
                        far_ref[:, kind, :, cols].reshape(part_rows, HD),
                    ],
                    axis=0,
                )
            )
        raws.append(
            lax.dot_general(
                keys[part],
                queries[part],
                (((1,), (1,)), ((), ())),
                preferred_element_type=jnp.float32,
            )
        )
        prob_grads.append(
            lax.dot_general(
                vals[part], grads[part], (((1,), (1,)), ((), ())), preferred_element_type=jnp.float32
            )
        )
    for part in parts:
        cols = slice(part * HD, (part + 1) * HD)
        query, grad = queries[part], grads[part]
        raw = jnp.minimum(raws[part], caps_ref[...])
        peak = jnp.max(raw, axis=0, keepdims=True)
        grown = jnp.exp2((raw - peak) * (factor * math.log2(math.e)))
        probs = grown * (1.0 / jnp.sum(grown, axis=0, keepdims=True))
        weights = probs.astype(jnp.bfloat16)
        attn = lax.dot_general(
            vals[part], weights, (((0,), (0,)), ((), ())), preferred_element_type=jnp.float32
        ).astype(jnp.bfloat16)
        attn_ref[:, cols] = attn.T
        row_dot = jnp.sum(probs * prob_grads[part], axis=0, keepdims=True)
        score_grads = (probs * (prob_grads[part] - row_dot)).astype(jnp.bfloat16)
        query_grad = lax.dot_general(
            keys[part], score_grads, (((0,), (0,)), ((), ())), preferred_element_type=jnp.float32
        )
        query_grad_ref[:, cols] = (query_grad * factor).astype(jnp.bfloat16).T
        key_terms = (
            jnp.dot(score_grads, query, preferred_element_type=jnp.float32) * factor
        ).astype(jnp.bfloat16)
        val_terms = jnp.dot(weights, grad, preferred_element_type=jnp.float32).astype(
            jnp.bfloat16
        )
        for kind, terms in enumerate((key_terms, val_terms)):
            local_ref[kind, :, cols] = terms[:rows_here]
            back_ref[kind, :, cols] = terms[rows_here : 2 * rows_here]
            first = 2 * rows_here
            near_grad_ref[:, kind, :, cols] = terms[first : first + half_rows].reshape(
                2 * slots, per_group, HD
            )
            far_grad_ref[:, kind, :, cols] = terms[first + half_rows :].reshape(
                2 * slots, per_group, HD
            )


def attention_call(
    caps,
    full,
    lower,
    summaries,
    first_col,
    summ_col,
    wide_done,
    round_width,
    round_col,
    round_done,
    after,
):
    rows_here, total_width = full[0].shape
    width = lower.shape[2]
    tile = math.gcd(width, 2 * HD)
    slots, _, per_group, _ = summaries[0].shape
    first = first_col // tile
    summ_first = summ_col // tile
    round_first = round_col // tile
    wide_spec = pl.BlockSpec((rows_here, tile), lambda i: (0, first + i))
    pair_spec = pl.BlockSpec((2, rows_here, tile), lambda i: (0, 0, i))
    summ_in = pl.BlockSpec((slots, 2, per_group, tile), lambda i: (0, 0, 0, summ_first + i))
    summ_out = pl.BlockSpec((2 * slots, 2, per_group, tile), lambda i: (0, 0, 0, round_first + i))
    wide = jax.ShapeDtypeStruct((rows_here, total_width), jnp.bfloat16)
    pair = jax.ShapeDtypeStruct((2, rows_here, width), jnp.bfloat16)
    summ = jax.ShapeDtypeStruct((2 * slots, 2, per_group, round_width), jnp.bfloat16)
    keys = caps.shape[0]
    heads = width // HD
    ahead = 6 + len(summaries)
    aliases = {ahead + i: i for i in range(len(wide_done))}
    aliases.update({ahead + len(wide_done) + i: 4 + i for i in range(len(round_done))})
    return pl.pallas_call(
        attention_step,
        grid=(width // tile,),
        in_specs=[pl.BlockSpec(caps.shape, lambda i: (0, 0))]
        + [wide_spec] * 4
        + [pair_spec]
        + [summ_in] * len(summaries)
        + [pl.BlockSpec(memory_space=pl.ANY)] * (len(aliases) + len(after)),
        out_specs=[wide_spec, wide_spec, pair_spec, pair_spec, summ_out, summ_out],
        out_shape=[wide, wide, pair, pair, summ, summ],
        input_output_aliases=aliases,
        compiler_params=pltpu.CompilerParams(vmem_limit_bytes=VMEM_GRANT),
        cost_estimate=pl.CostEstimate(
            flops=56 * heads * keys * rows_here * HD,
            bytes_accessed=heads * 16 * 2 * rows_here * HD,
            transcendentals=heads * keys * rows_here,
        ),
    )(caps, *full, lower, *summaries, *wide_done, *round_done, *after)


def finish_step(picker_ref, local_ref, back_ref, summ_ref, *rest):
    picker = picker_ref[...]
    for kind, out_ref in enumerate(rest[-2:]):
        spread = lax.dot_general(
            picker, summ_ref[kind], (((0,), (0,)), ((), ())), preferred_element_type=jnp.float32
        )
        total = local_ref[kind].astype(jnp.float32) + back_ref[kind].astype(jnp.float32)
        out_ref[...] = (total + spread).astype(jnp.bfloat16)


def finish_call(picker, local, back, summ, first_col, summ_col, total_width, carried):
    _, rows_here, width = local.shape
    tile = math.gcd(width, 4 * HD)
    first = first_col // tile
    summ_first = summ_col // tile
    few = summ.shape[1]
    pair_spec = pl.BlockSpec((2, rows_here, tile), lambda i: (0, 0, i))
    wide_spec = pl.BlockSpec((rows_here, tile), lambda i: (0, first + i))
    wide = jax.ShapeDtypeStruct((rows_here, total_width), jnp.bfloat16)
    any_spec = pl.BlockSpec(memory_space=pl.ANY)
    return pl.pallas_call(
        finish_step,
        grid=(width // tile,),
        in_specs=[
            pl.BlockSpec(picker.shape, lambda i: (0, 0)),
            pair_spec,
            pair_spec,
            pl.BlockSpec((2, few, tile), lambda i: (0, 0, summ_first + i)),
        ]
        + [any_spec] * len(carried),
        out_specs=[wide_spec, wide_spec],
        out_shape=[wide, wide],
        input_output_aliases={4 + i: i for i in range(len(carried))},
        compiler_params=pltpu.CompilerParams(vmem_limit_bytes=VMEM_GRANT),
        cost_estimate=pl.CostEstimate(
            flops=4 * few * rows_here * width,
            bytes_accessed=6 * 2 * rows_here * width,
            transcendentals=0,
        ),
    )(picker, local, back, summ, *carried)


def pick_step(picker_ref, key_ref, val_ref, out_ref):
    picker = picker_ref[...]
    for kind, ref in enumerate((key_ref, val_ref)):
        rows = jnp.dot(picker, ref[...], preferred_element_type=jnp.float32)
        out_ref[kind] = rows.astype(jnp.bfloat16)


def pick_call(picker, key_vectors, value_vectors):
    rows_here, total_width = key_vectors.shape
    few = picker.shape[0]
    tile = math.gcd(total_width, 8 * HD)
    wide_spec = pl.BlockSpec((rows_here, tile), lambda i: (0, i))
    return pl.pallas_call(
        pick_step,
        grid=(total_width // tile,),
        in_specs=[pl.BlockSpec(picker.shape, lambda i: (0, 0)), wide_spec, wide_spec],
        out_specs=pl.BlockSpec((2, few, tile), lambda i: (0, 0, i)),
        out_shape=jax.ShapeDtypeStruct((2, few, total_width), jnp.bfloat16),
        compiler_params=pltpu.CompilerParams(vmem_limit_bytes=VMEM_GRANT),
    )(picker, key_vectors, value_vectors)


def wait_for(array, other):
    zero = jnp.minimum(jnp.abs(other[(0,) * other.ndim].astype(jnp.float32)), 0.0)
    return array + zero.astype(array.dtype)


def add_rounded(*terms):
    total = terms[0].astype(jnp.float32)
    for term in terms[1:]:
        total = total + term.astype(jnp.float32)
    return total.astype(jnp.bfloat16)


def token_split(queries, key_vectors, value_vectors, out_grads, extra_blocks, summary_rows):
    rows_here, total_width = queries.shape
    seq_count = lax.axis_size("seq")
    stages = seq_count // 4
    group_id = lax.axis_index("seq")
    half = lax.axis_index("head")
    per_group = summary_rows.shape[1]
    few = per_group // 2
    flip_core = [(i, i ^ 1) for i in range(seq_count)]
    flip_side = [(i, i ^ 2) for i in range(seq_count)]
    flip_half = [(0, 1), (1, 0)]

    def climb(step):
        return [(i, i + 4 * step) for i in range(seq_count - 4 * step)]

    def descend(step):
        return [(i + 4 * step, i) for i in range(seq_count - 4 * step)]

    rows_mine = lax.dynamic_slice_in_dim(summary_rows[0], half * few, few, 0) - half * rows_here
    picker = (
        rows_mine[:, None] == jnp.arange(rows_here, dtype=jnp.int32)[None, :]
    ).astype(jnp.bfloat16)

    unit = total_width // 8
    chunks = [1, 2, 2, 2, 1]
    gather_rounds = [(0, 2), (2, 5)]
    reduce_rounds = [(0, 2), (2, 4), (4, 5)]
    edges = [sum(chunks[:i]) for i in range(len(chunks) + 1)]

    mine = pick_call(picker, key_vectors, value_vectors)
    other = lax.ppermute(mine, "head", flip_half)

    def lower_pair(chunk):
        cols = slice(edges[chunk] * unit, edges[chunk + 1] * unit)
        pair = jnp.stack([key_vectors[:, cols], value_vectors[:, cols]])
        return lax.ppermute(pair, "head", [(0, 1)])

    def gather(first, last, after, direct):
        cols = slice(edges[first] * unit, edges[last] * unit)
        ladder = jnp.concatenate([mine[:, :, cols], other[:, :, cols]], axis=1)[None]
        for item in after:
            ladder = wait_for(ladder, item)
        if direct:
            ladder = jnp.concatenate(
                [ladder] + [lax.ppermute(ladder, "seq", climb(i)) for i in range(1, stages)],
                axis=0,
            )
        size = ladder.shape[0]
        while size < stages:
            more = min(size, stages - size)
            ladder = jnp.concatenate(
                [ladder, lax.ppermute(ladder[:more], "seq", climb(size))], axis=0
            )
            size += more
        side = lax.ppermute(ladder, "seq", flip_side)
        return (
            ladder,
            side,
            lax.ppermute(ladder, "seq", flip_core),
            lax.ppermute(side, "seq", flip_core),
        )

    def reduce(near_grad, far_grad):
        chip = add_rounded(near_grad, lax.ppermute(far_grad, "seq", flip_core))
        plane = add_rounded(chip[:stages], lax.ppermute(chip[stages:], "seq", flip_side))
        sizes = [1]
        while sizes[-1] < stages:
            sizes.append(min(2 * sizes[-1], stages))
        for size, wider in zip(sizes[-2::-1], sizes[:0:-1]):
            more = wider - size
            moved = lax.ppermute(plane[size:wider], "seq", descend(size))
            head_part = add_rounded(plane[:more], moved)
            plane = (
                head_part
                if more == size
                else jnp.concatenate([head_part, plane[more:size]], axis=0)
            )
        group = plane[0]
        return add_rounded(group[:, :few], lax.ppermute(group[:, few:], "head", flip_half))

    caps = score_caps(extra_blocks[0], rows_here, half, group_id, stages, per_group)
    full = (queries, key_vectors, value_vectors, out_grads)

    lowers = [lower_pair(chunk) for chunk in range(len(chunks))]
    gathered = {}
    wide_done = ()
    finished = ()
    waiting = []
    backs = []
    summs = []
    for first, last in reduce_rounds:
        round_done = ()
        round_width = (edges[last] - edges[first]) * unit
        for chunk in range(first, last):
            if chunk == 0:
                gathered[0] = gather(*gather_rounds[0], (), True)
                begin, end = gather_rounds[1]
                gathered[begin] = gather(begin, end, (gathered[0][0],), False)
            gather_first = max(begin for begin in gathered if begin <= chunk)
            after = ((lowers[1],), (), backs[:1], backs[1:2], ())[chunk]
            out = attention_call(
                caps,
                full,
                lowers[chunk],
                gathered[gather_first],
                edges[chunk] * unit,
                (edges[chunk] - edges[gather_first]) * unit,
                wide_done,
                round_width,
                (edges[chunk] - edges[first]) * unit,
                round_done,
                after,
            )
            wide_done = tuple(out[:2])
            round_done = tuple(out[4:])
            back = lax.ppermute(out[3], "head", [(1, 0)])
            backs.append(back)
            waiting.append((chunk, out[2], back))
        summ = reduce(*round_done)
        summs.append(summ)
        for chunk, local, back in waiting:
            finished = finish_call(
                picker,
                local,
                back,
                summ,
                edges[chunk] * unit,
                (edges[chunk] - edges[first]) * unit,
                total_width,
                finished,
            )
        waiting = []
    return (*wide_done, *finished)


def solution(mesh):
    placed = (
        P(("seq", "head"), None),
        P(("seq", "head"), None),
        P(("seq", "head"), None),
        P(("seq", "head"), None),
        P("seq", None, None),
        P("seq", None),
    )
    paired = mesh.shape["head"] == 2 and mesh.shape["seq"] % 4 == 0
    return jax.shard_map(
        token_split if paired else per_device,
        mesh=mesh,
        in_specs=placed,
        out_specs=(
            P(("seq", "head"), None),
            P(("seq", "head"), None),
            P(("seq", "head"), None),
            P(("seq", "head"), None),
        ),
        check_vma=False,
    )
```

```python
import functools
import math

import jax
import jax.numpy as jnp
from jax import lax
from jax.experimental import pallas as pl
from jax.experimental.pallas import tpu as pltpu
from jax.sharding import PartitionSpec as P

HD = 128


neg_big = -1e30
pos_big = 3e38


def head_scores(query_heads, key_heads, factor):
    return (
        jnp.einsum("qhd,khd->hqk", query_heads, key_heads, preferred_element_type=jnp.float32)
        * factor
    )


def local_allowed(extra_map, group_len):
    block_count = extra_map.shape[0]
    block_len = group_len // block_count
    block_ids = jnp.arange(block_count, dtype=jnp.int32)
    block_lag = block_ids[:, None] - block_ids[None, :]
    allowed = (block_lag == 0) | (block_lag == 1) | (extra_map == 1) & (block_lag > 0)
    allowed = jnp.repeat(jnp.repeat(allowed, block_len, axis=0), block_len, axis=1)
    positions = jnp.arange(group_len, dtype=jnp.int32)
    return allowed & (positions[None, :] <= positions[:, None])


def key_window(summary_keys, summary_vals, block_id, key_rows, lower_end, upper_end, per_group):
    offset = block_id * key_rows
    key_block = lax.dynamic_slice_in_dim(summary_keys, offset, key_rows, 0)
    val_block = lax.dynamic_slice_in_dim(summary_vals, offset, key_rows, 0)
    owners = (offset + jnp.arange(key_rows, dtype=jnp.int32)) // per_group
    usable = (owners >= lower_end) & (owners < upper_end)
    return (offset, key_block, val_block, usable[None, None, :])


def block_bounds(lower_end, upper_end, key_rows, per_group):
    begin_block = lower_end * per_group // key_rows
    end_block = (upper_end * per_group + key_rows - 1) // key_rows
    return (begin_block, jnp.where(upper_end > lower_end, end_block, begin_block))


def softmax_stats(
    query_heads, summary_keys, summary_vals, lower_end, upper_end, key_rows, per_group, factor
):
    begin_block, end_block = block_bounds(lower_end, upper_end, key_rows, per_group)

    def softmax_advance(block_id, carried):
        peak, summed = carried
        offset, key_block, val_block, usable = key_window(
            summary_keys, summary_vals, block_id, key_rows, lower_end, upper_end, per_group
        )
        scores = jnp.where(usable, head_scores(query_heads, key_block, factor), neg_big)
        new_peak = jnp.maximum(peak, jnp.max(scores, axis=2))
        summed = summed * jnp.exp(peak - new_peak) + jnp.sum(
            jnp.exp(scores - new_peak[..., None]), axis=2
        )
        return (new_peak, summed)

    shape_hq = (query_heads.shape[1], query_heads.shape[0])
    start_stats = (jnp.full(shape_hq, neg_big, jnp.float32), jnp.zeros(shape_hq, jnp.float32))
    return lax.fori_loop(begin_block, end_block, softmax_advance, start_stats)


def merge_stats(earlier, later):
    peak = jnp.maximum(earlier[0], later[0])
    return (peak, earlier[1] * jnp.exp(earlier[0] - peak) + later[1] * jnp.exp(later[0] - peak))


def weighted_values(
    query_heads,
    log_mass,
    summary_keys,
    summary_vals,
    lower_end,
    upper_end,
    key_rows,
    per_group,
    factor,
):
    begin_block, end_block = block_bounds(lower_end, upper_end, key_rows, per_group)

    def weighted_advance(block_id, summed_values):
        offset, key_block, val_block, usable = key_window(
            summary_keys, summary_vals, block_id, key_rows, lower_end, upper_end, per_group
        )
        weights = jnp.where(
            usable, jnp.exp(head_scores(query_heads, key_block, factor) - log_mass[..., None]), 0.0
        ).astype(jnp.bfloat16)
        return summed_values + jnp.einsum(
            "hqk,khd->qhd", weights, val_block, preferred_element_type=jnp.float32
        )

    return lax.fori_loop(
        begin_block, end_block, weighted_advance, jnp.zeros(query_heads.shape, jnp.float32)
    )


def summary_backward(
    query_heads,
    grad_heads,
    log_mass,
    row_dot,
    summary_keys,
    summary_vals,
    lower_end,
    upper_end,
    key_rows,
    per_group,
    factor,
    carried,
):
    begin_block, end_block = block_bounds(lower_end, upper_end, key_rows, per_group)

    def summary_advance(block_id, running):
        query_acc, key_terms, val_terms = running
        offset, key_block, val_block, usable = key_window(
            summary_keys, summary_vals, block_id, key_rows, lower_end, upper_end, per_group
        )
        attn_probs = jnp.where(
            usable, jnp.exp(head_scores(query_heads, key_block, factor) - log_mass[..., None]), 0.0
        )
        weights = attn_probs.astype(jnp.bfloat16)
        prob_grads = jnp.einsum(
            "qhd,khd->hqk", grad_heads, val_block, preferred_element_type=jnp.float32
        )
        score_grads = (attn_probs * (prob_grads - row_dot[..., None])).astype(jnp.bfloat16)
        query_acc = (
            query_acc
            + jnp.einsum("hqk,khd->qhd", score_grads, key_block, preferred_element_type=jnp.float32)
            * factor
        )
        key_part = (
            jnp.einsum("hqk,qhd->khd", score_grads, query_heads, preferred_element_type=jnp.float32)
            * factor
        )
        val_part = jnp.einsum(
            "hqk,qhd->khd", weights, grad_heads, preferred_element_type=jnp.float32
        )
        key_terms = lax.dynamic_update_slice_in_dim(
            key_terms,
            lax.dynamic_slice_in_dim(key_terms, offset, key_rows, 0) + key_part,
            offset,
            0,
        )
        val_terms = lax.dynamic_update_slice_in_dim(
            val_terms,
            lax.dynamic_slice_in_dim(val_terms, offset, key_rows, 0) + val_part,
            offset,
            0,
        )
        return (query_acc, key_terms, val_terms)

    return lax.fori_loop(begin_block, end_block, summary_advance, carried)


def per_device(queries, key_vectors, value_vectors, out_grads, extra_blocks, summary_rows):
    query_all, key_all, val_all, grad_all = (
        lax.all_to_all(queries, "head", split_axis=1, concat_axis=0, tiled=True),
        lax.all_to_all(key_vectors, "head", split_axis=1, concat_axis=0, tiled=True),
        lax.all_to_all(value_vectors, "head", split_axis=1, concat_axis=0, tiled=True),
        lax.all_to_all(out_grads, "head", split_axis=1, concat_axis=0, tiled=True),
    )
    group_len, local_width = query_all.shape
    head_count = local_width // HD
    factor = HD ** (-0.5)
    query_heads = query_all.reshape(group_len, head_count, HD)
    key_heads = key_all.reshape(group_len, head_count, HD)
    val_heads = val_all.reshape(group_len, head_count, HD)
    grad_heads = grad_all.reshape(group_len, head_count, HD)
    per_group = summary_rows.shape[1]
    seq_count = lax.axis_size("seq")
    group_id = lax.axis_index("seq")
    picker = summary_rows[0][:, None] == jnp.arange(group_len, dtype=jnp.int32)[None, :]
    own_keys = jnp.dot(
        picker.astype(jnp.bfloat16), key_all, preferred_element_type=jnp.float32
    ).astype(jnp.bfloat16)
    own_vals = jnp.dot(
        picker.astype(jnp.bfloat16), val_all, preferred_element_type=jnp.float32
    ).astype(jnp.bfloat16)
    summ_keys_flat, summ_vals_flat = (
        lax.all_gather(own_keys, "seq", axis=0, tiled=True),
        lax.all_gather(own_vals, "seq", axis=0, tiled=True),
    )
    total_rows = summ_keys_flat.shape[0]
    summary_keys = summ_keys_flat.reshape(total_rows, head_count, HD)
    summary_vals = summ_vals_flat.reshape(total_rows, head_count, HD)
    key_rows = per_group * math.gcd(seq_count, max(1, 128 // per_group))
    allowed = local_allowed(extra_blocks[0], group_len)
    local_scores = jnp.where(allowed[None], head_scores(query_heads, key_heads, factor), neg_big)
    local_peak = jnp.max(local_scores, axis=2)
    local_stats = (local_peak, jnp.sum(jnp.exp(local_scores - local_peak[..., None]), axis=2))
    all_stats = merge_stats(
        local_stats,
        softmax_stats(
            query_heads, summary_keys, summary_vals, 0, group_id, key_rows, per_group, factor
        ),
    )
    log_mass = all_stats[0] + jnp.log(all_stats[1])
    summ_values = weighted_values(
        query_heads, log_mass, summary_keys, summary_vals, 0, group_id, key_rows, per_group, factor
    )
    local_probs = jnp.exp(local_scores - log_mass[..., None])
    local_weights = local_probs.astype(jnp.bfloat16)
    attention = (
        summ_values
        + jnp.einsum("hqk,khd->qhd", local_weights, val_heads, preferred_element_type=jnp.float32)
    ).astype(jnp.bfloat16)
    row_dot = jnp.einsum("qhd,qhd->hq", grad_heads, attention, preferred_element_type=jnp.float32)
    local_prob_grads = jnp.einsum(
        "qhd,khd->hqk", grad_heads, val_heads, preferred_element_type=jnp.float32
    )
    local_score_grads = (local_probs * (local_prob_grads - row_dot[..., None])).astype(jnp.bfloat16)
    query_local = (
        jnp.einsum("hqk,khd->qhd", local_score_grads, key_heads, preferred_element_type=jnp.float32)
        * factor
    )
    key_local = (
        jnp.einsum(
            "hqk,qhd->khd", local_score_grads, query_heads, preferred_element_type=jnp.float32
        )
        * factor
    )
    val_local = jnp.einsum(
        "hqk,qhd->khd", local_weights, grad_heads, preferred_element_type=jnp.float32
    )
    empty_terms = jnp.zeros((total_rows, head_count, HD), jnp.float32)
    start_running = (jnp.zeros(query_heads.shape, jnp.float32), empty_terms, empty_terms)
    query_summ, key_terms, val_terms = summary_backward(
        query_heads,
        grad_heads,
        log_mass,
        row_dot,
        summary_keys,
        summary_vals,
        0,
        group_id,
        key_rows,
        per_group,
        factor,
        start_running,
    )
    recv_keys, recv_vals = (
        lax.all_to_all(
            key_terms.astype(jnp.bfloat16), "seq", split_axis=0, concat_axis=0, tiled=True
        ).astype(key_terms.dtype),
        lax.all_to_all(
            val_terms.astype(jnp.bfloat16), "seq", split_axis=0, concat_axis=0, tiled=True
        ).astype(val_terms.dtype),
    )
    summ_key_grad = jnp.sum(recv_keys.reshape(seq_count, per_group, head_count, HD), axis=0)
    summ_val_grad = jnp.sum(recv_vals.reshape(seq_count, per_group, head_count, HD), axis=0)
    picker_f = picker.astype(jnp.float32)
    key_grad = key_local + jnp.einsum(
        "sq,shd->qhd", picker_f, summ_key_grad, precision=lax.Precision.HIGHEST
    )
    value_grad = val_local + jnp.einsum(
        "sq,shd->qhd", picker_f, summ_val_grad, precision=lax.Precision.HIGHEST
    )
    query_grad = query_local + query_summ
    outputs = (
        attention.reshape(group_len, local_width),
        query_grad.astype(jnp.bfloat16).reshape(group_len, local_width),
        key_grad.astype(jnp.bfloat16).reshape(group_len, local_width),
        value_grad.astype(jnp.bfloat16).reshape(group_len, local_width),
    )
    attention_out, query_out, key_out, value_out = (
        lax.all_to_all(outputs[0], "head", split_axis=0, concat_axis=1, tiled=True),
        lax.all_to_all(outputs[1], "head", split_axis=0, concat_axis=1, tiled=True),
        lax.all_to_all(outputs[2], "head", split_axis=0, concat_axis=1, tiled=True),
        lax.all_to_all(outputs[3], "head", split_axis=0, concat_axis=1, tiled=True),
    )
    return (attention_out, query_out, key_out, value_out)


VMEM_GRANT = 60 * 1024 * 1024


def caps_step(place_ref, usable_ref, extra_ref, caps_ref):
    rows_here = caps_ref.shape[1]
    mine = extra_ref.shape[0] // 2
    block_len = rows_here // mine
    half = place_ref[0]
    lane = lax.broadcasted_iota(jnp.int32, (block_len, rows_here), 1)
    row = lax.broadcasted_iota(jnp.int32, (block_len, rows_here), 0)
    lane_block = lane // block_len
    for part in range(2):
        for key_block in range(mine):
            group_block = key_block if part else half * mine + key_block
            allowed = jnp.zeros((block_len, rows_here), jnp.int32)
            for query_block in range(mine):
                lag = half * mine + query_block - group_block
                extra = extra_ref[half * mine + query_block, group_block]
                rule = jnp.where(
                    (lag == 0) | (lag == 1) | ((extra == 1) & (lag > 0)), jnp.int32(1), jnp.int32(0)
                )
                if part:
                    rule = rule * half
                allowed = jnp.where(lane_block == query_block, rule, allowed)
            caps = jnp.where(allowed == 1, pos_big, neg_big)
            if not part:
                caps = jnp.where(row + key_block * block_len <= lane, caps, neg_big)
            first = part * rows_here + key_block * block_len
            caps_ref[first : first + block_len, :] = caps
    slots = usable_ref.shape[0]
    per_group = (caps_ref.shape[0] - 2 * rows_here) // slots
    for slot in range(slots):
        first = 2 * rows_here + slot * per_group
        caps_ref[first : first + per_group, :] = jnp.full(
            (per_group, rows_here), jnp.where(usable_ref[slot] == 1, pos_big, neg_big), jnp.float32
        )


def caps_call(half, usable, extra_map, rows_here, per_group):
    keys = 2 * rows_here + usable.shape[0] * per_group
    smem = pl.BlockSpec(memory_space=pltpu.SMEM)
    return pl.pallas_call(
        caps_step,
        in_specs=[smem] * 3,
        out_shape=jax.ShapeDtypeStruct((keys, rows_here), jnp.float32),
        compiler_params=pltpu.CompilerParams(vmem_limit_bytes=VMEM_GRANT),
    )(half[None], usable, extra_map)


def summary_slots(group_id, stages):
    d_core = jnp.arange(2, dtype=jnp.int32)[:, None, None]
    d_side = jnp.arange(2, dtype=jnp.int32)[None, :, None]
    level = group_id // 4 - jnp.arange(stages, dtype=jnp.int32)[None, None, :]
    side = (group_id // 2 + d_side) % 2
    owner = level * 4 + side * 2 + (group_id + d_core) % 2
    return ((level >= 0) & (owner < group_id)).astype(jnp.int32).reshape(-1)


def attention_step(
    summ_parts,
    caps_ref,
    query_ref,
    key_ref,
    val_ref,
    grad_ref,
    lower_ref,
    *rest,
):
    attn_ref, query_grad_ref, local_ref, back_ref, *summ_grad_refs, mark_ref = rest[-7:]
    mark_ref[...] = jnp.zeros(mark_ref.shape, mark_ref.dtype)
    rows_here, width = query_ref.shape
    part_slots, _, per_group, _ = rest[0].shape
    part_rows = part_slots * per_group
    half_slots = summ_parts * part_slots // 2
    half_rows = half_slots * per_group

    def summary(kind, cols):
        return [ref[:, kind, :, cols].reshape(part_rows, HD) for ref in rest[:summ_parts]]

    factor = HD ** (-0.5)
    parts = range(width // HD)
    queries, grads, keys, vals, raws, prob_grads = [], [], [], [], [], []
    for part in parts:
        cols = slice(part * HD, (part + 1) * HD)
        queries.append(query_ref[:, cols])
        grads.append(grad_ref[:, cols])
        for kind, (own_ref, into) in enumerate(((key_ref, keys), (val_ref, vals))):
            into.append(
                jnp.concatenate(
                    [
                        own_ref[:, cols],
                        lower_ref[kind, :, cols],
                        *summary(kind, cols),
                    ],
                    axis=0,
                )
            )
        raws.append(
            lax.dot_general(
                keys[part],
                queries[part],
                (((1,), (1,)), ((), ())),
                preferred_element_type=jnp.float32,
            )
        )
        prob_grads.append(
            lax.dot_general(
                vals[part], grads[part], (((1,), (1,)), ((), ())), preferred_element_type=jnp.float32
            )
        )
    for part in parts:
        cols = slice(part * HD, (part + 1) * HD)
        query, grad = queries[part], grads[part]
        raw = jnp.minimum(raws[part], caps_ref[...])
        peak = jnp.max(raw, axis=0, keepdims=True)
        grown = jnp.exp2((raw - peak) * (factor * math.log2(math.e)))
        probs = grown * (1.0 / jnp.sum(grown, axis=0, keepdims=True))
        weights = probs.astype(jnp.bfloat16)
        attn = lax.dot_general(
            vals[part], weights, (((0,), (0,)), ((), ())), preferred_element_type=jnp.float32
        ).astype(jnp.bfloat16)
        attn_ref[:, cols] = attn.T
        row_dot = jnp.sum(probs * prob_grads[part], axis=0, keepdims=True)
        score_grads = (probs * (prob_grads[part] - row_dot)).astype(jnp.bfloat16)
        query_grad = lax.dot_general(
            keys[part], score_grads, (((0,), (0,)), ((), ())), preferred_element_type=jnp.float32
        )
        query_grad_ref[:, cols] = (query_grad * factor).astype(jnp.bfloat16).T
        key_terms = (
            jnp.dot(score_grads, query, preferred_element_type=jnp.float32) * factor
        ).astype(jnp.bfloat16)
        val_terms = jnp.dot(weights, grad, preferred_element_type=jnp.float32).astype(
            jnp.bfloat16
        )
        for kind, terms in enumerate((key_terms, val_terms)):
            local_ref[kind, :, cols] = terms[:rows_here]
            back_ref[kind, :, cols] = terms[rows_here : 2 * rows_here]
            first = 2 * rows_here
            for i, ref in enumerate(summ_grad_refs):
                begin = first + i * half_rows
                ref[:, kind, :, cols] = terms[begin : begin + half_rows].reshape(
                    half_slots, per_group, HD
                )


def attention_call(
    caps,
    full,
    lower,
    width,
    lower_col,
    summaries,
    first_col,
    summ_col,
    wide_done,
    round_width,
    round_col,
    round_done,
    after,
):
    rows_here, total_width = full[0].shape
    tile = math.gcd(width, 2 * HD)
    slots, _, per_group, _ = summaries[0].shape
    half_slots = len(summaries) * slots // 2
    first = first_col // tile
    summ_first = summ_col // tile
    lower_first = lower_col // tile
    round_first = round_col // tile
    wide_spec = pl.BlockSpec((rows_here, tile), lambda i: (0, first + i))
    pair_spec = pl.BlockSpec((2, rows_here, tile), lambda i: (0, 0, i))
    summ_in = pl.BlockSpec((slots, 2, per_group, tile), lambda i: (0, 0, 0, summ_first + i))
    summ_out = pl.BlockSpec(
        (half_slots, 2, per_group, tile), lambda i: (0, 0, 0, round_first + i)
    )
    wide = jax.ShapeDtypeStruct((rows_here, total_width), jnp.bfloat16)
    pair = jax.ShapeDtypeStruct((2, rows_here, width), jnp.bfloat16)
    wide_pair = jax.ShapeDtypeStruct((2, rows_here, total_width), jnp.bfloat16)
    wide_pair_spec = pl.BlockSpec((2, rows_here, tile), lambda i: (0, 0, first + i))
    summ = jax.ShapeDtypeStruct((half_slots, 2, per_group, round_width), jnp.bfloat16)
    mark = jax.ShapeDtypeStruct((per_group, total_width // 2), jnp.bfloat16)
    keys = caps.shape[0]
    heads = width // HD
    ahead = 6 + len(summaries)
    aliases = {ahead + i: i for i in range(len(wide_done))}
    aliases.update({ahead + len(wide_done) + i: 4 + i for i in range(len(round_done))})
    return pl.pallas_call(
        functools.partial(attention_step, len(summaries)),
        grid=(width // tile,),
        in_specs=[pl.BlockSpec(caps.shape, lambda i: (0, 0))]
        + [wide_spec] * 4
        + [pl.BlockSpec((2, rows_here, tile), lambda i: (0, 0, lower_first + i))]
        + [summ_in] * len(summaries)
        + [pl.BlockSpec(memory_space=pl.ANY)] * (len(aliases) + len(after)),
        out_specs=[
            wide_spec,
            wide_spec,
            wide_pair_spec,
            pair_spec,
            summ_out,
            summ_out,
            pl.BlockSpec(mark.shape, lambda i: (0, 0)),
        ],
        out_shape=[wide, wide, wide_pair, pair, summ, summ, mark],
        input_output_aliases=aliases,
        compiler_params=pltpu.CompilerParams(vmem_limit_bytes=VMEM_GRANT),
        cost_estimate=pl.CostEstimate(
            flops=56 * heads * keys * rows_here * HD,
            bytes_accessed=heads * 16 * 2 * rows_here * HD,
            transcendentals=heads * keys * rows_here,
        ),
    )(caps, *full, lower, *summaries, *wide_done, *round_done, *after)


def finish_step(bounds, picker_ref, summ_ref, local_ref, *refs):
    outs = refs[-2:]
    count = len(bounds) - 1
    step = pl.program_id(0)
    picker = picker_ref[...]
    for part in range(count):

        @pl.when((step >= bounds[part]) & (step < bounds[part + 1]))
        def _():
            back_ref = refs[part]
            for kind, out_ref in enumerate(outs):
                spread = lax.dot_general(
                    picker,
                    summ_ref[kind],
                    (((0,), (0,)), ((), ())),
                    preferred_element_type=jnp.float32,
                )
                total = local_ref[kind].astype(jnp.float32) + back_ref[kind].astype(jnp.float32)
                out_ref[...] = (total + spread).astype(jnp.bfloat16)


def finish_call(picker, summ, local, backs):
    rows_here = picker.shape[1]
    few, total_width = summ.shape[1:]
    tile = functools.reduce(math.gcd, [part.shape[2] for part in backs], 4 * HD)
    bounds = [sum(part.shape[2] for part in backs[:i]) // tile for i in range(len(backs) + 1)]

    def part_spec(part):
        low, high = bounds[part], bounds[part + 1]
        return pl.BlockSpec(
            (2, rows_here, tile), lambda i: (0, 0, jnp.clip(i - low, 0, high - low - 1))
        )

    specs = [part_spec(part) for part in range(len(backs))]
    wide_spec = pl.BlockSpec((rows_here, tile), lambda i: (0, i))
    wide = jax.ShapeDtypeStruct((rows_here, total_width), jnp.bfloat16)
    return pl.pallas_call(
        functools.partial(finish_step, bounds),
        grid=(bounds[-1],),
        in_specs=[
            pl.BlockSpec(picker.shape, lambda i: (0, 0)),
            pl.BlockSpec((2, few, tile), lambda i: (0, 0, i)),
        ]
        + [pl.BlockSpec((2, rows_here, tile), lambda i: (0, 0, i))]
        + specs,
        out_specs=[wide_spec, wide_spec],
        out_shape=[wide, wide],
        compiler_params=pltpu.CompilerParams(vmem_limit_bytes=VMEM_GRANT),
        cost_estimate=pl.CostEstimate(
            flops=4 * few * rows_here * total_width,
            bytes_accessed=6 * 2 * rows_here * total_width,
            transcendentals=0,
        ),
    )(picker, summ, local, *backs)


def pick_step(place_ref, rows_ref, key_ref, val_ref, out_ref, picker_ref):
    few, rows_here = picker_ref.shape
    half = place_ref[0]
    row = lax.broadcasted_iota(jnp.int32, (few, rows_here), 0)
    wanted = jnp.full((few, rows_here), -1, jnp.int32)
    for i in range(few):
        wanted = jnp.where(row == i, rows_ref[0, half * few + i] - half * rows_here, wanted)
    hit = lax.broadcasted_iota(jnp.int32, (few, rows_here), 1) == wanted
    picker = jnp.where(hit, 1.0, 0.0).astype(jnp.bfloat16)
    picker_ref[...] = picker
    for kind, ref in enumerate((key_ref, val_ref)):
        rows = jnp.dot(picker, ref[...], preferred_element_type=jnp.float32)
        out_ref[kind] = rows.astype(jnp.bfloat16)


def pick_call(half, summary_rows, key_vectors, value_vectors):
    rows_here, total_width = key_vectors.shape
    few = summary_rows.shape[1] // 2
    tile = math.gcd(total_width, 8 * HD)
    wide_spec = pl.BlockSpec((rows_here, tile), lambda i: (0, i))
    smem = pl.BlockSpec(memory_space=pltpu.SMEM)
    return pl.pallas_call(
        pick_step,
        grid=(total_width // tile,),
        in_specs=[smem, smem, wide_spec, wide_spec],
        out_specs=[
            pl.BlockSpec((2, few, tile), lambda i: (0, 0, i)),
            pl.BlockSpec((few, rows_here), lambda i: (0, 0)),
        ],
        out_shape=[
            jax.ShapeDtypeStruct((2, few, total_width), jnp.bfloat16),
            jax.ShapeDtypeStruct((few, rows_here), jnp.bfloat16),
        ],
        compiler_params=pltpu.CompilerParams(vmem_limit_bytes=VMEM_GRANT),
    )(half[None], summary_rows, key_vectors, value_vectors)


def wait_for(array, mark):
    return array + mark[:, : array.shape[-1]]


def wait_for_moved(array, moved):
    return array + jnp.minimum(jnp.abs(moved[0, :1, :1]), 0)


def add_rounded(*terms):
    total = terms[0].astype(jnp.float32)
    for term in terms[1:]:
        total = total + term.astype(jnp.float32)
    return total.astype(jnp.bfloat16)


def token_split(queries, key_vectors, value_vectors, out_grads, extra_blocks, summary_rows):
    rows_here, total_width = queries.shape
    seq_count = lax.axis_size("seq")
    stages = seq_count // 4
    group_id = lax.axis_index("seq")
    half = lax.axis_index("head")
    per_group = summary_rows.shape[1]
    few = per_group // 2
    flip_core = [(i, i ^ 1) for i in range(seq_count)]
    flip_side = [(i, i ^ 2) for i in range(seq_count)]
    flip_half = [(0, 1), (1, 0)]

    def climb(step):
        return [(i, i + 4 * step) for i in range(seq_count - 4 * step)]

    def descend(step):
        return [(i + 4 * step, i) for i in range(seq_count - 4 * step)]

    unit = total_width // 8
    chunks = [1, 3, 2, 2]
    gather_starts = [0, 2]
    edges = [sum(chunks[:i]) for i in range(len(chunks) + 1)]

    mine, picker = pick_call(half, summary_rows, key_vectors, value_vectors)
    other = lax.ppermute(mine, "head", flip_half)

    def lower_pair(first, last, zeros=None):
        cols = slice(edges[first] * unit, edges[last] * unit)
        pair = jnp.stack([key_vectors[:, cols], value_vectors[:, cols]])
        if zeros is not None:
            pair = pair + zeros[:1, : pair.shape[2]]
        lowers.append(lax.ppermute(pair, "head", [(0, 1)]))
        lower_starts.append(first)

    both = jnp.concatenate([mine, other], axis=1)

    def span(first, last):
        return slice(edges[first] * unit, edges[last] * unit)

    def climb_stages(first, last):
        ladder = both[:, :, span(first, last)][None]
        return jnp.concatenate(
            [ladder] + [lax.ppermute(ladder, "seq", climb(i)) for i in range(1, stages)], axis=0
        )

    def with_other_core(near):
        return near, lax.ppermute(near, "seq", flip_core)

    def reduce_chip(near_grad, far_grad):
        return add_rounded(near_grad, lax.ppermute(far_grad, "seq", flip_core))

    def reduce_plane(chip):
        return add_rounded(chip[:stages], lax.ppermute(chip[stages:], "seq", flip_side))

    def reduce_group(plane):
        return add_rounded(
            plane[0],
            *[lax.ppermute(plane[i], "seq", descend(i)) for i in range(1, stages)],
        )

    def reduce_group_halving(plane):
        while plane.shape[0] > 1 and plane.shape[0] % 2 == 0:
            size = plane.shape[0] // 2
            plane = add_rounded(plane[:size], lax.ppermute(plane[size:], "seq", descend(size)))
        return reduce_group(plane) if plane.shape[0] > 1 else plane[0]

    def reduce_half(groups):
        group = jnp.concatenate(groups, axis=2)
        return add_rounded(group[:, :few], lax.ppermute(group[:, few:], "head", flip_half))

    usable = summary_slots(group_id, stages)
    caps = caps_call(half, usable, extra_blocks[0], rows_here, per_group)
    full = (queries, key_vectors, value_vectors, out_grads)

    lowers = []
    lower_starts = []
    gathered = []
    marks = []
    wide_done = ()
    backs = []

    def attend(chunk, source, reduce_first, reduce_last, round_done, after):
        nonlocal wide_done
        low = max(start for start in lower_starts if start <= chunk)
        out = attention_call(
            caps,
            full,
            lowers[lower_starts.index(low)],
            (edges[chunk + 1] - edges[chunk]) * unit,
            (edges[chunk] - edges[low]) * unit,
            gathered[source],
            edges[chunk] * unit,
            (edges[chunk] - edges[gather_starts[source]]) * unit,
            wide_done,
            (edges[reduce_last] - edges[reduce_first]) * unit,
            (edges[chunk] - edges[reduce_first]) * unit,
            round_done,
            after,
        )
        wide_done = tuple(out[:3])
        backs.append(lax.ppermute(out[3], "head", [(1, 0)]))
        marks.append(out[-1])
        return tuple(out[4:-1])


    lower_pair(0, 2)
    ladder = climb_stages(0, 2)
    side = lax.ppermute(ladder, "seq", flip_side)
    lower_pair(2, 3, jnp.minimum(jnp.abs(side[0, 0]), 0))
    gathered.append(with_other_core(jnp.concatenate([ladder, side], axis=0)))
    ladder = climb_stages(2, 4)
    side = lax.ppermute(ladder, "seq", flip_side)
    done = attend(0, 0, 0, 2, (), ())
    lower_pair(3, 4, marks[0])
    near = wait_for(jnp.concatenate([ladder, side], axis=0), marks[0])
    gathered.append(with_other_core(near))
    done = attend(1, 0, 0, 2, done, ())
    chip_a = reduce_chip(*done)
    done = attend(2, 1, 2, 3, (), (backs[0],))
    chip_a = wait_for(chip_a, marks[2])
    plane_a = reduce_plane(chip_a)
    chip_b = reduce_chip(*done)
    done = attend(3, 1, 3, 4, (), (backs[1], chip_a))
    chip_b = wait_for(chip_b, marks[3])
    plane_b = reduce_plane(chip_b)
    chip_c = wait_for_moved(reduce_chip(*done), backs[2])
    plane_c = reduce_plane(chip_c)
    group_a = reduce_group_halving(plane_a)
    group_b = reduce_group(jnp.concatenate([plane_b, plane_c], axis=3))
    group_b = wait_for_moved(group_b, backs[3])
    finished = finish_call(picker, reduce_half([group_a, group_b]), wide_done[2], backs)
    return (*wide_done[:2], *finished)


def solution(mesh):
    placed = (
        P(("seq", "head"), None),
        P(("seq", "head"), None),
        P(("seq", "head"), None),
        P(("seq", "head"), None),
        P("seq", None, None),
        P("seq", None),
    )
    paired = mesh.shape["head"] == 2 and mesh.shape["seq"] % 4 == 0
    return jax.shard_map(
        token_split if paired else per_device,
        mesh=mesh,
        in_specs=placed,
        out_specs=(
            P(("seq", "head"), None),
            P(("seq", "head"), None),
            P(("seq", "head"), None),
            P(("seq", "head"), None),
        ),
        check_vma=False,
    )
```

```python
import functools
import math

import jax
import jax.numpy as jnp
from jax import lax
from jax.experimental import pallas as pl
from jax.experimental.pallas import tpu as pltpu
from jax.sharding import PartitionSpec as P

HD = 128


neg_big = -1e30
pos_big = 3e38


def head_scores(query_heads, key_heads, factor):
    return (
        jnp.einsum("qhd,khd->hqk", query_heads, key_heads, preferred_element_type=jnp.float32)
        * factor
    )


def local_allowed(extra_map, group_len):
    block_count = extra_map.shape[0]
    block_len = group_len // block_count
    block_ids = jnp.arange(block_count, dtype=jnp.int32)
    block_lag = block_ids[:, None] - block_ids[None, :]
    allowed = (block_lag == 0) | (block_lag == 1) | (extra_map == 1) & (block_lag > 0)
    allowed = jnp.repeat(jnp.repeat(allowed, block_len, axis=0), block_len, axis=1)
    positions = jnp.arange(group_len, dtype=jnp.int32)
    return allowed & (positions[None, :] <= positions[:, None])


def key_window(summary_keys, summary_vals, block_id, key_rows, lower_end, upper_end, per_group):
    offset = block_id * key_rows
    key_block = lax.dynamic_slice_in_dim(summary_keys, offset, key_rows, 0)
    val_block = lax.dynamic_slice_in_dim(summary_vals, offset, key_rows, 0)
    owners = (offset + jnp.arange(key_rows, dtype=jnp.int32)) // per_group
    usable = (owners >= lower_end) & (owners < upper_end)
    return (offset, key_block, val_block, usable[None, None, :])


def block_bounds(lower_end, upper_end, key_rows, per_group):
    begin_block = lower_end * per_group // key_rows
    end_block = (upper_end * per_group + key_rows - 1) // key_rows
    return (begin_block, jnp.where(upper_end > lower_end, end_block, begin_block))


def softmax_stats(
    query_heads, summary_keys, summary_vals, lower_end, upper_end, key_rows, per_group, factor
):
    begin_block, end_block = block_bounds(lower_end, upper_end, key_rows, per_group)

    def softmax_advance(block_id, carried):
        peak, summed = carried
        offset, key_block, val_block, usable = key_window(
            summary_keys, summary_vals, block_id, key_rows, lower_end, upper_end, per_group
        )
        scores = jnp.where(usable, head_scores(query_heads, key_block, factor), neg_big)
        new_peak = jnp.maximum(peak, jnp.max(scores, axis=2))
        summed = summed * jnp.exp(peak - new_peak) + jnp.sum(
            jnp.exp(scores - new_peak[..., None]), axis=2
        )
        return (new_peak, summed)

    shape_hq = (query_heads.shape[1], query_heads.shape[0])
    start_stats = (jnp.full(shape_hq, neg_big, jnp.float32), jnp.zeros(shape_hq, jnp.float32))
    return lax.fori_loop(begin_block, end_block, softmax_advance, start_stats)


def merge_stats(earlier, later):
    peak = jnp.maximum(earlier[0], later[0])
    return (peak, earlier[1] * jnp.exp(earlier[0] - peak) + later[1] * jnp.exp(later[0] - peak))


def weighted_values(
    query_heads,
    log_mass,
    summary_keys,
    summary_vals,
    lower_end,
    upper_end,
    key_rows,
    per_group,
    factor,
):
    begin_block, end_block = block_bounds(lower_end, upper_end, key_rows, per_group)

    def weighted_advance(block_id, summed_values):
        offset, key_block, val_block, usable = key_window(
            summary_keys, summary_vals, block_id, key_rows, lower_end, upper_end, per_group
        )
        weights = jnp.where(
            usable, jnp.exp(head_scores(query_heads, key_block, factor) - log_mass[..., None]), 0.0
        ).astype(jnp.bfloat16)
        return summed_values + jnp.einsum(
            "hqk,khd->qhd", weights, val_block, preferred_element_type=jnp.float32
        )

    return lax.fori_loop(
        begin_block, end_block, weighted_advance, jnp.zeros(query_heads.shape, jnp.float32)
    )


def summary_backward(
    query_heads,
    grad_heads,
    log_mass,
    row_dot,
    summary_keys,
    summary_vals,
    lower_end,
    upper_end,
    key_rows,
    per_group,
    factor,
    carried,
):
    begin_block, end_block = block_bounds(lower_end, upper_end, key_rows, per_group)

    def summary_advance(block_id, running):
        query_acc, key_terms, val_terms = running
        offset, key_block, val_block, usable = key_window(
            summary_keys, summary_vals, block_id, key_rows, lower_end, upper_end, per_group
        )
        attn_probs = jnp.where(
            usable, jnp.exp(head_scores(query_heads, key_block, factor) - log_mass[..., None]), 0.0
        )
        weights = attn_probs.astype(jnp.bfloat16)
        prob_grads = jnp.einsum(
            "qhd,khd->hqk", grad_heads, val_block, preferred_element_type=jnp.float32
        )
        score_grads = (attn_probs * (prob_grads - row_dot[..., None])).astype(jnp.bfloat16)
        query_acc = (
            query_acc
            + jnp.einsum("hqk,khd->qhd", score_grads, key_block, preferred_element_type=jnp.float32)
            * factor
        )
        key_part = (
            jnp.einsum("hqk,qhd->khd", score_grads, query_heads, preferred_element_type=jnp.float32)
            * factor
        )
        val_part = jnp.einsum(
            "hqk,qhd->khd", weights, grad_heads, preferred_element_type=jnp.float32
        )
        key_terms = lax.dynamic_update_slice_in_dim(
            key_terms,
            lax.dynamic_slice_in_dim(key_terms, offset, key_rows, 0) + key_part,
            offset,
            0,
        )
        val_terms = lax.dynamic_update_slice_in_dim(
            val_terms,
            lax.dynamic_slice_in_dim(val_terms, offset, key_rows, 0) + val_part,
            offset,
            0,
        )
        return (query_acc, key_terms, val_terms)

    return lax.fori_loop(begin_block, end_block, summary_advance, carried)


def per_device(queries, key_vectors, value_vectors, out_grads, extra_blocks, summary_rows):
    query_all, key_all, val_all, grad_all = (
        lax.all_to_all(queries, "head", split_axis=1, concat_axis=0, tiled=True),
        lax.all_to_all(key_vectors, "head", split_axis=1, concat_axis=0, tiled=True),
        lax.all_to_all(value_vectors, "head", split_axis=1, concat_axis=0, tiled=True),
        lax.all_to_all(out_grads, "head", split_axis=1, concat_axis=0, tiled=True),
    )
    group_len, local_width = query_all.shape
    head_count = local_width // HD
    factor = HD ** (-0.5)
    query_heads = query_all.reshape(group_len, head_count, HD)
    key_heads = key_all.reshape(group_len, head_count, HD)
    val_heads = val_all.reshape(group_len, head_count, HD)
    grad_heads = grad_all.reshape(group_len, head_count, HD)
    per_group = summary_rows.shape[1]
    seq_count = lax.axis_size("seq")
    group_id = lax.axis_index("seq")
    picker = summary_rows[0][:, None] == jnp.arange(group_len, dtype=jnp.int32)[None, :]
    own_keys = jnp.dot(
        picker.astype(jnp.bfloat16), key_all, preferred_element_type=jnp.float32
    ).astype(jnp.bfloat16)
    own_vals = jnp.dot(
        picker.astype(jnp.bfloat16), val_all, preferred_element_type=jnp.float32
    ).astype(jnp.bfloat16)
    summ_keys_flat, summ_vals_flat = (
        lax.all_gather(own_keys, "seq", axis=0, tiled=True),
        lax.all_gather(own_vals, "seq", axis=0, tiled=True),
    )
    total_rows = summ_keys_flat.shape[0]
    summary_keys = summ_keys_flat.reshape(total_rows, head_count, HD)
    summary_vals = summ_vals_flat.reshape(total_rows, head_count, HD)
    key_rows = per_group * math.gcd(seq_count, max(1, 128 // per_group))
    allowed = local_allowed(extra_blocks[0], group_len)
    local_scores = jnp.where(allowed[None], head_scores(query_heads, key_heads, factor), neg_big)
    local_peak = jnp.max(local_scores, axis=2)
    local_stats = (local_peak, jnp.sum(jnp.exp(local_scores - local_peak[..., None]), axis=2))
    all_stats = merge_stats(
        local_stats,
        softmax_stats(
            query_heads, summary_keys, summary_vals, 0, group_id, key_rows, per_group, factor
        ),
    )
    log_mass = all_stats[0] + jnp.log(all_stats[1])
    summ_values = weighted_values(
        query_heads, log_mass, summary_keys, summary_vals, 0, group_id, key_rows, per_group, factor
    )
    local_probs = jnp.exp(local_scores - log_mass[..., None])
    local_weights = local_probs.astype(jnp.bfloat16)
    attention = (
        summ_values
        + jnp.einsum("hqk,khd->qhd", local_weights, val_heads, preferred_element_type=jnp.float32)
    ).astype(jnp.bfloat16)
    row_dot = jnp.einsum("qhd,qhd->hq", grad_heads, attention, preferred_element_type=jnp.float32)
    local_prob_grads = jnp.einsum(
        "qhd,khd->hqk", grad_heads, val_heads, preferred_element_type=jnp.float32
    )
    local_score_grads = (local_probs * (local_prob_grads - row_dot[..., None])).astype(jnp.bfloat16)
    query_local = (
        jnp.einsum("hqk,khd->qhd", local_score_grads, key_heads, preferred_element_type=jnp.float32)
        * factor
    )
    key_local = (
        jnp.einsum(
            "hqk,qhd->khd", local_score_grads, query_heads, preferred_element_type=jnp.float32
        )
        * factor
    )
    val_local = jnp.einsum(
        "hqk,qhd->khd", local_weights, grad_heads, preferred_element_type=jnp.float32
    )
    empty_terms = jnp.zeros((total_rows, head_count, HD), jnp.float32)
    start_running = (jnp.zeros(query_heads.shape, jnp.float32), empty_terms, empty_terms)
    query_summ, key_terms, val_terms = summary_backward(
        query_heads,
        grad_heads,
        log_mass,
        row_dot,
        summary_keys,
        summary_vals,
        0,
        group_id,
        key_rows,
        per_group,
        factor,
        start_running,
    )
    recv_keys, recv_vals = (
        lax.all_to_all(
            key_terms.astype(jnp.bfloat16), "seq", split_axis=0, concat_axis=0, tiled=True
        ).astype(key_terms.dtype),
        lax.all_to_all(
            val_terms.astype(jnp.bfloat16), "seq", split_axis=0, concat_axis=0, tiled=True
        ).astype(val_terms.dtype),
    )
    summ_key_grad = jnp.sum(recv_keys.reshape(seq_count, per_group, head_count, HD), axis=0)
    summ_val_grad = jnp.sum(recv_vals.reshape(seq_count, per_group, head_count, HD), axis=0)
    picker_f = picker.astype(jnp.float32)
    key_grad = key_local + jnp.einsum(
        "sq,shd->qhd", picker_f, summ_key_grad, precision=lax.Precision.HIGHEST
    )
    value_grad = val_local + jnp.einsum(
        "sq,shd->qhd", picker_f, summ_val_grad, precision=lax.Precision.HIGHEST
    )
    query_grad = query_local + query_summ
    outputs = (
        attention.reshape(group_len, local_width),
        query_grad.astype(jnp.bfloat16).reshape(group_len, local_width),
        key_grad.astype(jnp.bfloat16).reshape(group_len, local_width),
        value_grad.astype(jnp.bfloat16).reshape(group_len, local_width),
    )
    attention_out, query_out, key_out, value_out = (
        lax.all_to_all(outputs[0], "head", split_axis=0, concat_axis=1, tiled=True),
        lax.all_to_all(outputs[1], "head", split_axis=0, concat_axis=1, tiled=True),
        lax.all_to_all(outputs[2], "head", split_axis=0, concat_axis=1, tiled=True),
        lax.all_to_all(outputs[3], "head", split_axis=0, concat_axis=1, tiled=True),
    )
    return (attention_out, query_out, key_out, value_out)


VMEM_GRANT = 60 * 1024 * 1024


def caps_step(place_ref, usable_ref, extra_ref, caps_ref):
    rows_here = caps_ref.shape[1]
    mine = extra_ref.shape[0] // 2
    block_len = rows_here // mine
    half = place_ref[0]
    lane = lax.broadcasted_iota(jnp.int32, (block_len, rows_here), 1)
    row = lax.broadcasted_iota(jnp.int32, (block_len, rows_here), 0)
    lane_block = lane // block_len
    for part in range(2):
        for key_block in range(mine):
            group_block = key_block if part else half * mine + key_block
            allowed = jnp.zeros((block_len, rows_here), jnp.int32)
            for query_block in range(mine):
                lag = half * mine + query_block - group_block
                extra = extra_ref[half * mine + query_block, group_block]
                rule = jnp.where(
                    (lag == 0) | (lag == 1) | ((extra == 1) & (lag > 0)), jnp.int32(1), jnp.int32(0)
                )
                if part:
                    rule = rule * half
                allowed = jnp.where(lane_block == query_block, rule, allowed)
            caps = jnp.where(allowed == 1, pos_big, neg_big)
            if not part:
                caps = jnp.where(row + key_block * block_len <= lane, caps, neg_big)
            first = part * rows_here + key_block * block_len
            caps_ref[first : first + block_len, :] = caps
    slots = usable_ref.shape[0]
    per_group = (caps_ref.shape[0] - 2 * rows_here) // slots
    for slot in range(slots):
        first = 2 * rows_here + slot * per_group
        caps_ref[first : first + per_group, :] = jnp.full(
            (per_group, rows_here), jnp.where(usable_ref[slot] == 1, pos_big, neg_big), jnp.float32
        )


def caps_call(half, usable, extra_map, rows_here, per_group):
    keys = 2 * rows_here + usable.shape[0] * per_group
    smem = pl.BlockSpec(memory_space=pltpu.SMEM)
    return pl.pallas_call(
        caps_step,
        in_specs=[smem] * 3,
        out_shape=jax.ShapeDtypeStruct((keys, rows_here), jnp.float32),
        compiler_params=pltpu.CompilerParams(vmem_limit_bytes=VMEM_GRANT),
    )(half[None], usable, extra_map)


def summary_slots(group_id, stages):
    d_core = jnp.arange(2, dtype=jnp.int32)[:, None, None]
    d_side = jnp.arange(2, dtype=jnp.int32)[None, :, None]
    level = group_id // 4 - jnp.arange(stages, dtype=jnp.int32)[None, None, :]
    side = (group_id // 2 + d_side) % 2
    owner = level * 4 + side * 2 + (group_id + d_core) % 2
    return ((level >= 0) & (owner < group_id)).astype(jnp.int32).reshape(-1)


def attention_step(
    summ_parts,
    caps_ref,
    query_ref,
    key_ref,
    val_ref,
    grad_ref,
    lower_ref,
    *rest,
):
    attn_ref, query_grad_ref, local_ref, back_ref, *summ_grad_refs, mark_ref = rest[-7:]
    mark_ref[...] = jnp.zeros(mark_ref.shape, mark_ref.dtype)
    rows_here, width = query_ref.shape
    part_slots, _, per_group, _ = rest[0].shape
    part_rows = part_slots * per_group
    half_slots = summ_parts * part_slots // 2
    half_rows = half_slots * per_group

    def summary(kind, cols):
        return [ref[:, kind, :, cols].reshape(part_rows, HD) for ref in rest[:summ_parts]]

    factor = HD ** (-0.5)
    parts = range(width // HD)
    queries, grads, keys, vals, raws, prob_grads = [], [], [], [], [], []
    for part in parts:
        cols = slice(part * HD, (part + 1) * HD)
        queries.append(query_ref[:, cols])
        grads.append(grad_ref[:, cols])
        for kind, (own_ref, into) in enumerate(((key_ref, keys), (val_ref, vals))):
            into.append(
                jnp.concatenate(
                    [
                        own_ref[:, cols],
                        lower_ref[kind, :, cols],
                        *summary(kind, cols),
                    ],
                    axis=0,
                )
            )
        raws.append(
            lax.dot_general(
                keys[part],
                queries[part],
                (((1,), (1,)), ((), ())),
                preferred_element_type=jnp.float32,
            )
        )
        prob_grads.append(
            lax.dot_general(
                vals[part], grads[part], (((1,), (1,)), ((), ())), preferred_element_type=jnp.float32
            )
        )
    for part in parts:
        cols = slice(part * HD, (part + 1) * HD)
        query, grad = queries[part], grads[part]
        raw = jnp.minimum(raws[part], caps_ref[...])
        peak = jnp.max(raw, axis=0, keepdims=True)
        grown = jnp.exp2((raw - peak) * (factor * math.log2(math.e)))
        probs = grown * (1.0 / jnp.sum(grown, axis=0, keepdims=True))
        weights = probs.astype(jnp.bfloat16)
        attn = lax.dot_general(
            vals[part], weights, (((0,), (0,)), ((), ())), preferred_element_type=jnp.float32
        ).astype(jnp.bfloat16)
        attn_ref[:, cols] = attn.T
        row_dot = jnp.sum(probs * prob_grads[part], axis=0, keepdims=True)
        score_grads = (probs * (prob_grads[part] - row_dot)).astype(jnp.bfloat16)
        query_grad = lax.dot_general(
            keys[part], score_grads, (((0,), (0,)), ((), ())), preferred_element_type=jnp.float32
        )
        query_grad_ref[:, cols] = (query_grad * factor).astype(jnp.bfloat16).T
        key_terms = (
            jnp.dot(score_grads, query, preferred_element_type=jnp.float32) * factor
        ).astype(jnp.bfloat16)
        val_terms = jnp.dot(weights, grad, preferred_element_type=jnp.float32).astype(
            jnp.bfloat16
        )
        for kind, terms in enumerate((key_terms, val_terms)):
            local_ref[kind, :, cols] = terms[:rows_here]
            back_ref[kind, :, cols] = terms[rows_here : 2 * rows_here]
            first = 2 * rows_here
            for i, ref in enumerate(summ_grad_refs):
                begin = first + i * half_rows
                ref[:, kind, :, cols] = terms[begin : begin + half_rows].reshape(
                    half_slots, per_group, HD
                )


def attention_call(
    caps,
    full,
    lower,
    width,
    lower_col,
    summaries,
    first_col,
    summ_col,
    wide_done,
    round_width,
    round_col,
    round_done,
    after,
):
    rows_here, total_width = full[0].shape
    tile = math.gcd(width, 2 * HD)
    slots, _, per_group, _ = summaries[0].shape
    half_slots = len(summaries) * slots // 2
    first = first_col // tile
    summ_first = summ_col // tile
    lower_first = lower_col // tile
    round_first = round_col // tile
    wide_spec = pl.BlockSpec((rows_here, tile), lambda i: (0, first + i))
    pair_spec = pl.BlockSpec((2, rows_here, tile), lambda i: (0, 0, i))
    summ_in = pl.BlockSpec((slots, 2, per_group, tile), lambda i: (0, 0, 0, summ_first + i))
    summ_out = pl.BlockSpec(
        (half_slots, 2, per_group, tile), lambda i: (0, 0, 0, round_first + i)
    )
    wide = jax.ShapeDtypeStruct((rows_here, total_width), jnp.bfloat16)
    pair = jax.ShapeDtypeStruct((2, rows_here, width), jnp.bfloat16)
    wide_pair = jax.ShapeDtypeStruct((2, rows_here, total_width), jnp.bfloat16)
    wide_pair_spec = pl.BlockSpec((2, rows_here, tile), lambda i: (0, 0, first + i))
    summ = jax.ShapeDtypeStruct((half_slots, 2, per_group, round_width), jnp.bfloat16)
    mark = jax.ShapeDtypeStruct((per_group, 5 * total_width // 8), jnp.bfloat16)
    keys = caps.shape[0]
    heads = width // HD
    ahead = 6 + len(summaries)
    aliases = {ahead + i: i for i in range(len(wide_done))}
    aliases.update({ahead + len(wide_done) + i: 4 + i for i in range(len(round_done))})
    return pl.pallas_call(
        functools.partial(attention_step, len(summaries)),
        grid=(width // tile,),
        in_specs=[pl.BlockSpec(caps.shape, lambda i: (0, 0))]
        + [wide_spec] * 4
        + [pl.BlockSpec((2, rows_here, tile), lambda i: (0, 0, lower_first + i))]
        + [summ_in] * len(summaries)
        + [pl.BlockSpec(memory_space=pl.ANY)] * (len(aliases) + len(after)),
        out_specs=[
            wide_spec,
            wide_spec,
            wide_pair_spec,
            pair_spec,
            summ_out,
            summ_out,
            pl.BlockSpec(mark.shape, lambda i: (0, 0)),
        ],
        out_shape=[wide, wide, wide_pair, pair, summ, summ, mark],
        input_output_aliases=aliases,
        compiler_params=pltpu.CompilerParams(vmem_limit_bytes=VMEM_GRANT),
        cost_estimate=pl.CostEstimate(
            flops=56 * heads * keys * rows_here * HD,
            bytes_accessed=heads * 16 * 2 * rows_here * HD,
            transcendentals=heads * keys * rows_here,
        ),
    )(caps, *full, lower, *summaries, *wide_done, *round_done, *after)


def merge_step(bounds, local_ref, *refs):
    outs = refs[-2:]
    step = pl.program_id(0)
    for part in range(len(bounds) - 1):

        @pl.when((step >= bounds[part]) & (step < bounds[part + 1]))
        def _():
            for kind, out_ref in enumerate(outs):
                total = local_ref[kind].astype(jnp.float32) + refs[part][kind].astype(jnp.float32)
                out_ref[...] = total.astype(jnp.bfloat16)


def merge_call(local, backs, first_col, carried):
    _, rows_here, total_width = local.shape
    tile = functools.reduce(math.gcd, [part.shape[2] for part in backs], 4 * HD)
    first = first_col // tile
    bounds = [sum(part.shape[2] for part in backs[:i]) // tile for i in range(len(backs) + 1)]

    def part_spec(part):
        low, high = bounds[part], bounds[part + 1]
        return pl.BlockSpec(
            (2, rows_here, tile), lambda i: (0, 0, jnp.clip(i - low, 0, high - low - 1))
        )

    wide_spec = pl.BlockSpec((rows_here, tile), lambda i: (0, first + i))
    wide = jax.ShapeDtypeStruct((rows_here, total_width), jnp.bfloat16)
    return pl.pallas_call(
        functools.partial(merge_step, bounds),
        grid=(bounds[-1],),
        in_specs=[pl.BlockSpec((2, rows_here, tile), lambda i: (0, 0, first + i))]
        + [part_spec(part) for part in range(len(backs))]
        + [pl.BlockSpec(memory_space=pl.ANY)] * len(carried),
        out_specs=[wide_spec, wide_spec],
        out_shape=[wide, wide],
        input_output_aliases={1 + len(backs) + i: i for i in range(len(carried))},
        compiler_params=pltpu.CompilerParams(vmem_limit_bytes=VMEM_GRANT),
        cost_estimate=pl.CostEstimate(
            flops=2 * rows_here * tile * bounds[-1],
            bytes_accessed=12 * rows_here * tile * bounds[-1],
            transcendentals=0,
        ),
    )(local, *backs, *carried)


def place_step(rows_ref, summ_ref, key_ref, val_ref, key_out_ref, val_out_ref, tiles, sems):
    _, few, tile, _ = tiles.shape

    def copies(refs, back):
        for kind, ref in enumerate(refs):
            for step in range(few):
                first = pl.multiple_of(rows_ref[step] // tile * tile, tile)
                there = ref.at[pl.ds(first, tile), :]
                here = tiles.at[kind, step]
                yield pltpu.make_async_copy(
                    here if back else there, there if back else here, sems.at[kind, step]
                )

    for copy in copies((key_ref, val_ref), False):
        copy.start()
    for copy in copies((key_ref, val_ref), False):
        copy.wait()
    row = lax.broadcasted_iota(jnp.int32, (tile, few), 0)
    slot = lax.broadcasted_iota(jnp.int32, (tile, few), 1)
    for step in range(few):
        place = lax.rem(rows_ref[step], tile)
        spread = jnp.where((row == place) & (slot == step), 1.0, 0.0).astype(jnp.bfloat16)
        for kind in range(2):
            moved = jnp.dot(spread, summ_ref[kind], preferred_element_type=jnp.float32)
            total = tiles[kind, step].astype(jnp.float32) + moved
            tiles[kind, step] = total.astype(jnp.bfloat16)
    for copy in copies((key_out_ref, val_out_ref), True):
        copy.start()
    for copy in copies((key_out_ref, val_out_ref), True):
        copy.wait()


def place_call(rows, summ, key_grad, val_grad):
    _, few, total_width = summ.shape
    any_spec = pl.BlockSpec(memory_space=pl.ANY)
    wide = jax.ShapeDtypeStruct(key_grad.shape, key_grad.dtype)
    return pl.pallas_call(
        place_step,
        in_specs=[
            pl.BlockSpec(memory_space=pltpu.SMEM),
            pl.BlockSpec(memory_space=pltpu.VMEM),
            any_spec,
            any_spec,
        ],
        out_specs=[any_spec, any_spec],
        out_shape=[wide, wide],
        scratch_shapes=[
            pltpu.VMEM((2, few, 16, total_width), jnp.bfloat16),
            pltpu.SemaphoreType.DMA((2, few)),
        ],
        input_output_aliases={2: 0, 3: 1},
        compiler_params=pltpu.CompilerParams(vmem_limit_bytes=VMEM_GRANT),
        cost_estimate=pl.CostEstimate(
            flops=64 * few * few * total_width,
            bytes_accessed=128 * few * total_width,
            transcendentals=0,
        ),
    )(rows, summ, key_grad, val_grad)


def pick_step(place_ref, rows_ref, key_ref, val_ref, out_ref):
    few, rows_here = out_ref.shape[1], key_ref.shape[0]
    half = place_ref[0]
    row = lax.broadcasted_iota(jnp.int32, (few, rows_here), 0)
    wanted = jnp.full((few, rows_here), -1, jnp.int32)
    for i in range(few):
        wanted = jnp.where(row == i, rows_ref[0, half * few + i] - half * rows_here, wanted)
    hit = lax.broadcasted_iota(jnp.int32, (few, rows_here), 1) == wanted
    picker = jnp.where(hit, 1.0, 0.0).astype(jnp.bfloat16)
    for kind, ref in enumerate((key_ref, val_ref)):
        rows = jnp.dot(picker, ref[...], preferred_element_type=jnp.float32)
        out_ref[kind] = rows.astype(jnp.bfloat16)


def pick_call(half, summary_rows, key_vectors, value_vectors):
    rows_here, total_width = key_vectors.shape
    few = summary_rows.shape[1] // 2
    tile = math.gcd(total_width, 8 * HD)
    wide_spec = pl.BlockSpec((rows_here, tile), lambda i: (0, i))
    smem = pl.BlockSpec(memory_space=pltpu.SMEM)
    return pl.pallas_call(
        pick_step,
        grid=(total_width // tile,),
        in_specs=[smem, smem, wide_spec, wide_spec],
        out_specs=pl.BlockSpec((2, few, tile), lambda i: (0, 0, i)),
        out_shape=jax.ShapeDtypeStruct((2, few, total_width), jnp.bfloat16),
        compiler_params=pltpu.CompilerParams(vmem_limit_bytes=VMEM_GRANT),
    )(half[None], summary_rows, key_vectors, value_vectors)


def wait_for(array, mark):
    return array + mark[:, : array.shape[-1]]


def wait_for_moved(array, moved):
    return array + jnp.minimum(jnp.abs(moved[0, :1, :1]), 0)


def add_rounded(*terms):
    total = terms[0].astype(jnp.float32)
    for term in terms[1:]:
        total = total + term.astype(jnp.float32)
    return total.astype(jnp.bfloat16)


def token_split(queries, key_vectors, value_vectors, out_grads, extra_blocks, summary_rows):
    rows_here, total_width = queries.shape
    seq_count = lax.axis_size("seq")
    stages = seq_count // 4
    group_id = lax.axis_index("seq")
    half = lax.axis_index("head")
    per_group = summary_rows.shape[1]
    few = per_group // 2
    flip_core = [(i, i ^ 1) for i in range(seq_count)]
    flip_side = [(i, i ^ 2) for i in range(seq_count)]
    flip_half = [(0, 1), (1, 0)]

    def climb(step):
        return [(i, i + 4 * step) for i in range(seq_count - 4 * step)]

    def descend(step):
        return [(i + 4 * step, i) for i in range(seq_count - 4 * step)]

    unit = total_width // 8
    chunks = [1, 2, 3, 2]
    gather_starts = [0, 2]
    edges = [sum(chunks[:i]) for i in range(len(chunks) + 1)]

    mine = pick_call(half, summary_rows, key_vectors, value_vectors)
    other = lax.ppermute(mine, "head", flip_half)

    def lower_pair(first, last, zeros=None):
        cols = slice(edges[first] * unit, edges[last] * unit)
        pair = jnp.stack([key_vectors[:, cols], value_vectors[:, cols]])
        if zeros is not None:
            pair = pair + zeros[:1, : pair.shape[2]]
        lowers.append(lax.ppermute(pair, "head", [(0, 1)]))
        lower_starts.append(first)

    both = jnp.concatenate([mine, other], axis=1)

    def span(first, last):
        return slice(edges[first] * unit, edges[last] * unit)

    def climb_stages(first, last, before=None):
        ladder = both[:, :, span(first, last)][None]
        if before is not None:
            ladder = ladder + jnp.minimum(jnp.abs(before[1, :1, :1, :1]), 0)
        return jnp.concatenate(
            [ladder] + [lax.ppermute(ladder, "seq", climb(i)) for i in range(1, stages)], axis=0
        )

    def with_other_core(near):
        return near, lax.ppermute(near, "seq", flip_core)

    def reduce_chip(near_grad, far_grad):
        return add_rounded(near_grad, lax.ppermute(far_grad, "seq", flip_core))

    def reduce_plane(chip):
        return add_rounded(chip[:stages], lax.ppermute(chip[stages:], "seq", flip_side))

    def reduce_group(plane):
        return add_rounded(
            plane[0],
            *[lax.ppermute(plane[i], "seq", descend(i)) for i in range(1, stages)],
        )

    def reduce_group_halving(plane):
        while plane.shape[0] > 1 and plane.shape[0] % 2 == 0:
            size = plane.shape[0] // 2
            plane = add_rounded(plane[:size], lax.ppermute(plane[size:], "seq", descend(size)))
        return reduce_group(plane) if plane.shape[0] > 1 else plane[0]

    def reduce_half(groups):
        group = jnp.concatenate(groups, axis=2)
        return add_rounded(group[:, :few], lax.ppermute(group[:, few:], "head", flip_half))

    usable = summary_slots(group_id, stages)
    caps = caps_call(half, usable, extra_blocks[0], rows_here, per_group)
    full = (queries, key_vectors, value_vectors, out_grads)

    lowers = []
    lower_starts = []
    gathered = []
    marks = []
    wide_done = ()
    backs = []

    def attend(chunk, source, reduce_first, reduce_last, round_done, after):
        nonlocal wide_done
        low = max(start for start in lower_starts if start <= chunk)
        out = attention_call(
            caps,
            full,
            lowers[lower_starts.index(low)],
            (edges[chunk + 1] - edges[chunk]) * unit,
            (edges[chunk] - edges[low]) * unit,
            gathered[source],
            edges[chunk] * unit,
            (edges[chunk] - edges[gather_starts[source]]) * unit,
            wide_done,
            (edges[reduce_last] - edges[reduce_first]) * unit,
            (edges[chunk] - edges[reduce_first]) * unit,
            round_done,
            after,
        )
        wide_done = tuple(out[:3])
        backs.append(lax.ppermute(out[3], "head", [(1, 0)]))
        marks.append(out[-1])
        return tuple(out[4:-1])

    rows_mine = lax.dynamic_slice_in_dim(summary_rows[0], half * few, few, 0) - half * rows_here

    lower_pair(0, 2)
    ladder = climb_stages(0, 2)
    first_ladder = ladder
    side = lax.ppermute(ladder, "seq", flip_side)
    lower_pair(2, 3, jnp.minimum(jnp.abs(side[0, 0]), 0))
    gathered.append(with_other_core(jnp.concatenate([ladder, side], axis=0)))
    ladder = climb_stages(2, 4, first_ladder)
    done = attend(0, 0, 0, 2, (), ())
    lower_pair(3, 4, marks[0])
    ladder = wait_for(ladder, marks[0])
    side = lax.ppermute(ladder, "seq", flip_side)
    done = attend(1, 0, 0, 2, done, ())
    near = wait_for(jnp.concatenate([ladder, side], axis=0), marks[1])
    near = wait_for_moved(near, backs[0])
    gathered.append(with_other_core(near))
    chip_a = reduce_chip(*done)
    done = attend(2, 1, 2, 3, (), ())
    chip_a = wait_for(chip_a, marks[2])
    plane_a = reduce_plane(chip_a)
    chip_b = reduce_chip(*done)
    done = attend(3, 1, 3, 4, (), (backs[1], chip_a))
    chip_b = wait_for(chip_b, marks[3])
    plane_b = reduce_plane(chip_b)
    chip_c = wait_for_moved(reduce_chip(*done), backs[2])
    plane_c = reduce_plane(chip_c)
    group_a = reduce_group_halving(plane_a)
    merged = merge_call(wide_done[2], backs[:3], 0, ())
    plane_b = wait_for_moved(jnp.concatenate([plane_b, plane_c], axis=3), merged[0][None])
    group_b = wait_for_moved(reduce_group(plane_b), backs[3])
    merged = merge_call(wide_done[2], backs[3:], edges[3] * unit, tuple(merged))
    finished = place_call(rows_mine, reduce_half([group_a, group_b]), *merged)
    return (*wide_done[:2], *finished)


def solution(mesh):
    placed = (
        P(("seq", "head"), None),
        P(("seq", "head"), None),
        P(("seq", "head"), None),
        P(("seq", "head"), None),
        P("seq", None, None),
        P("seq", None),
    )
    paired = mesh.shape["head"] == 2 and mesh.shape["seq"] % 4 == 0
    return jax.shard_map(
        token_split if paired else per_device,
        mesh=mesh,
        in_specs=placed,
        out_specs=(
            P(("seq", "head"), None),
            P(("seq", "head"), None),
            P(("seq", "head"), None),
            P(("seq", "head"), None),
        ),
        check_vma=False,
    )
```

```python
import functools
import math

import jax
import jax.numpy as jnp
from jax import lax
from jax.experimental import pallas as pl
from jax.experimental.pallas import tpu as pltpu
from jax.sharding import PartitionSpec as P

HD = 128


neg_big = -1e30
pos_big = 3e38


def head_scores(query_heads, key_heads, factor):
    return (
        jnp.einsum("qhd,khd->hqk", query_heads, key_heads, preferred_element_type=jnp.float32)
        * factor
    )


def local_allowed(extra_map, group_len):
    block_count = extra_map.shape[0]
    block_len = group_len // block_count
    block_ids = jnp.arange(block_count, dtype=jnp.int32)
    block_lag = block_ids[:, None] - block_ids[None, :]
    allowed = (block_lag == 0) | (block_lag == 1) | (extra_map == 1) & (block_lag > 0)
    allowed = jnp.repeat(jnp.repeat(allowed, block_len, axis=0), block_len, axis=1)
    positions = jnp.arange(group_len, dtype=jnp.int32)
    return allowed & (positions[None, :] <= positions[:, None])


def key_window(summary_keys, summary_vals, block_id, key_rows, lower_end, upper_end, per_group):
    offset = block_id * key_rows
    key_block = lax.dynamic_slice_in_dim(summary_keys, offset, key_rows, 0)
    val_block = lax.dynamic_slice_in_dim(summary_vals, offset, key_rows, 0)
    owners = (offset + jnp.arange(key_rows, dtype=jnp.int32)) // per_group
    usable = (owners >= lower_end) & (owners < upper_end)
    return (offset, key_block, val_block, usable[None, None, :])


def block_bounds(lower_end, upper_end, key_rows, per_group):
    begin_block = lower_end * per_group // key_rows
    end_block = (upper_end * per_group + key_rows - 1) // key_rows
    return (begin_block, jnp.where(upper_end > lower_end, end_block, begin_block))


def softmax_stats(
    query_heads, summary_keys, summary_vals, lower_end, upper_end, key_rows, per_group, factor
):
    begin_block, end_block = block_bounds(lower_end, upper_end, key_rows, per_group)

    def softmax_advance(block_id, carried):
        peak, summed = carried
        offset, key_block, val_block, usable = key_window(
            summary_keys, summary_vals, block_id, key_rows, lower_end, upper_end, per_group
        )
        scores = jnp.where(usable, head_scores(query_heads, key_block, factor), neg_big)
        new_peak = jnp.maximum(peak, jnp.max(scores, axis=2))
        summed = summed * jnp.exp(peak - new_peak) + jnp.sum(
            jnp.exp(scores - new_peak[..., None]), axis=2
        )
        return (new_peak, summed)

    shape_hq = (query_heads.shape[1], query_heads.shape[0])
    start_stats = (jnp.full(shape_hq, neg_big, jnp.float32), jnp.zeros(shape_hq, jnp.float32))
    return lax.fori_loop(begin_block, end_block, softmax_advance, start_stats)


def merge_stats(earlier, later):
    peak = jnp.maximum(earlier[0], later[0])
    return (peak, earlier[1] * jnp.exp(earlier[0] - peak) + later[1] * jnp.exp(later[0] - peak))


def weighted_values(
    query_heads,
    log_mass,
    summary_keys,
    summary_vals,
    lower_end,
    upper_end,
    key_rows,
    per_group,
    factor,
):
    begin_block, end_block = block_bounds(lower_end, upper_end, key_rows, per_group)

    def weighted_advance(block_id, summed_values):
        offset, key_block, val_block, usable = key_window(
            summary_keys, summary_vals, block_id, key_rows, lower_end, upper_end, per_group
        )
        weights = jnp.where(
            usable, jnp.exp(head_scores(query_heads, key_block, factor) - log_mass[..., None]), 0.0
        ).astype(jnp.bfloat16)
        return summed_values + jnp.einsum(
            "hqk,khd->qhd", weights, val_block, preferred_element_type=jnp.float32
        )

    return lax.fori_loop(
        begin_block, end_block, weighted_advance, jnp.zeros(query_heads.shape, jnp.float32)
    )


def summary_backward(
    query_heads,
    grad_heads,
    log_mass,
    row_dot,
    summary_keys,
    summary_vals,
    lower_end,
    upper_end,
    key_rows,
    per_group,
    factor,
    carried,
):
    begin_block, end_block = block_bounds(lower_end, upper_end, key_rows, per_group)

    def summary_advance(block_id, running):
        query_acc, key_terms, val_terms = running
        offset, key_block, val_block, usable = key_window(
            summary_keys, summary_vals, block_id, key_rows, lower_end, upper_end, per_group
        )
        attn_probs = jnp.where(
            usable, jnp.exp(head_scores(query_heads, key_block, factor) - log_mass[..., None]), 0.0
        )
        weights = attn_probs.astype(jnp.bfloat16)
        prob_grads = jnp.einsum(
            "qhd,khd->hqk", grad_heads, val_block, preferred_element_type=jnp.float32
        )
        score_grads = (attn_probs * (prob_grads - row_dot[..., None])).astype(jnp.bfloat16)
        query_acc = (
            query_acc
            + jnp.einsum("hqk,khd->qhd", score_grads, key_block, preferred_element_type=jnp.float32)
            * factor
        )
        key_part = (
            jnp.einsum("hqk,qhd->khd", score_grads, query_heads, preferred_element_type=jnp.float32)
            * factor
        )
        val_part = jnp.einsum(
            "hqk,qhd->khd", weights, grad_heads, preferred_element_type=jnp.float32
        )
        key_terms = lax.dynamic_update_slice_in_dim(
            key_terms,
            lax.dynamic_slice_in_dim(key_terms, offset, key_rows, 0) + key_part,
            offset,
            0,
        )
        val_terms = lax.dynamic_update_slice_in_dim(
            val_terms,
            lax.dynamic_slice_in_dim(val_terms, offset, key_rows, 0) + val_part,
            offset,
            0,
        )
        return (query_acc, key_terms, val_terms)

    return lax.fori_loop(begin_block, end_block, summary_advance, carried)


def per_device(queries, key_vectors, value_vectors, out_grads, extra_blocks, summary_rows):
    query_all, key_all, val_all, grad_all = (
        lax.all_to_all(queries, "head", split_axis=1, concat_axis=0, tiled=True),
        lax.all_to_all(key_vectors, "head", split_axis=1, concat_axis=0, tiled=True),
        lax.all_to_all(value_vectors, "head", split_axis=1, concat_axis=0, tiled=True),
        lax.all_to_all(out_grads, "head", split_axis=1, concat_axis=0, tiled=True),
    )
    group_len, local_width = query_all.shape
    head_count = local_width // HD
    factor = HD ** (-0.5)
    query_heads = query_all.reshape(group_len, head_count, HD)
    key_heads = key_all.reshape(group_len, head_count, HD)
    val_heads = val_all.reshape(group_len, head_count, HD)
    grad_heads = grad_all.reshape(group_len, head_count, HD)
    per_group = summary_rows.shape[1]
    seq_count = lax.axis_size("seq")
    group_id = lax.axis_index("seq")
    picker = summary_rows[0][:, None] == jnp.arange(group_len, dtype=jnp.int32)[None, :]
    own_keys = jnp.dot(
        picker.astype(jnp.bfloat16), key_all, preferred_element_type=jnp.float32
    ).astype(jnp.bfloat16)
    own_vals = jnp.dot(
        picker.astype(jnp.bfloat16), val_all, preferred_element_type=jnp.float32
    ).astype(jnp.bfloat16)
    summ_keys_flat, summ_vals_flat = (
        lax.all_gather(own_keys, "seq", axis=0, tiled=True),
        lax.all_gather(own_vals, "seq", axis=0, tiled=True),
    )
    total_rows = summ_keys_flat.shape[0]
    summary_keys = summ_keys_flat.reshape(total_rows, head_count, HD)
    summary_vals = summ_vals_flat.reshape(total_rows, head_count, HD)
    key_rows = per_group * math.gcd(seq_count, max(1, 128 // per_group))
    allowed = local_allowed(extra_blocks[0], group_len)
    local_scores = jnp.where(allowed[None], head_scores(query_heads, key_heads, factor), neg_big)
    local_peak = jnp.max(local_scores, axis=2)
    local_stats = (local_peak, jnp.sum(jnp.exp(local_scores - local_peak[..., None]), axis=2))
    all_stats = merge_stats(
        local_stats,
        softmax_stats(
            query_heads, summary_keys, summary_vals, 0, group_id, key_rows, per_group, factor
        ),
    )
    log_mass = all_stats[0] + jnp.log(all_stats[1])
    summ_values = weighted_values(
        query_heads, log_mass, summary_keys, summary_vals, 0, group_id, key_rows, per_group, factor
    )
    local_probs = jnp.exp(local_scores - log_mass[..., None])
    local_weights = local_probs.astype(jnp.bfloat16)
    attention = (
        summ_values
        + jnp.einsum("hqk,khd->qhd", local_weights, val_heads, preferred_element_type=jnp.float32)
    ).astype(jnp.bfloat16)
    row_dot = jnp.einsum("qhd,qhd->hq", grad_heads, attention, preferred_element_type=jnp.float32)
    local_prob_grads = jnp.einsum(
        "qhd,khd->hqk", grad_heads, val_heads, preferred_element_type=jnp.float32
    )
    local_score_grads = (local_probs * (local_prob_grads - row_dot[..., None])).astype(jnp.bfloat16)
    query_local = (
        jnp.einsum("hqk,khd->qhd", local_score_grads, key_heads, preferred_element_type=jnp.float32)
        * factor
    )
    key_local = (
        jnp.einsum(
            "hqk,qhd->khd", local_score_grads, query_heads, preferred_element_type=jnp.float32
        )
        * factor
    )
    val_local = jnp.einsum(
        "hqk,qhd->khd", local_weights, grad_heads, preferred_element_type=jnp.float32
    )
    empty_terms = jnp.zeros((total_rows, head_count, HD), jnp.float32)
    start_running = (jnp.zeros(query_heads.shape, jnp.float32), empty_terms, empty_terms)
    query_summ, key_terms, val_terms = summary_backward(
        query_heads,
        grad_heads,
        log_mass,
        row_dot,
        summary_keys,
        summary_vals,
        0,
        group_id,
        key_rows,
        per_group,
        factor,
        start_running,
    )
    recv_keys, recv_vals = (
        lax.all_to_all(
            key_terms.astype(jnp.bfloat16), "seq", split_axis=0, concat_axis=0, tiled=True
        ).astype(key_terms.dtype),
        lax.all_to_all(
            val_terms.astype(jnp.bfloat16), "seq", split_axis=0, concat_axis=0, tiled=True
        ).astype(val_terms.dtype),
    )
    summ_key_grad = jnp.sum(recv_keys.reshape(seq_count, per_group, head_count, HD), axis=0)
    summ_val_grad = jnp.sum(recv_vals.reshape(seq_count, per_group, head_count, HD), axis=0)
    picker_f = picker.astype(jnp.float32)
    key_grad = key_local + jnp.einsum(
        "sq,shd->qhd", picker_f, summ_key_grad, precision=lax.Precision.HIGHEST
    )
    value_grad = val_local + jnp.einsum(
        "sq,shd->qhd", picker_f, summ_val_grad, precision=lax.Precision.HIGHEST
    )
    query_grad = query_local + query_summ
    outputs = (
        attention.reshape(group_len, local_width),
        query_grad.astype(jnp.bfloat16).reshape(group_len, local_width),
        key_grad.astype(jnp.bfloat16).reshape(group_len, local_width),
        value_grad.astype(jnp.bfloat16).reshape(group_len, local_width),
    )
    attention_out, query_out, key_out, value_out = (
        lax.all_to_all(outputs[0], "head", split_axis=0, concat_axis=1, tiled=True),
        lax.all_to_all(outputs[1], "head", split_axis=0, concat_axis=1, tiled=True),
        lax.all_to_all(outputs[2], "head", split_axis=0, concat_axis=1, tiled=True),
        lax.all_to_all(outputs[3], "head", split_axis=0, concat_axis=1, tiled=True),
    )
    return (attention_out, query_out, key_out, value_out)


VMEM_GRANT = 60 * 1024 * 1024


def caps_step(place_ref, usable_ref, extra_ref, caps_ref):
    rows_here = caps_ref.shape[1]
    mine = extra_ref.shape[0] // 2
    block_len = rows_here // mine
    half = place_ref[0]
    lane = lax.broadcasted_iota(jnp.int32, (block_len, rows_here), 1)
    row = lax.broadcasted_iota(jnp.int32, (block_len, rows_here), 0)
    lane_block = lane // block_len
    for part in range(2):
        for key_block in range(mine):
            group_block = key_block if part else half * mine + key_block
            allowed = jnp.zeros((block_len, rows_here), jnp.int32)
            for query_block in range(mine):
                lag = half * mine + query_block - group_block
                extra = extra_ref[half * mine + query_block, group_block]
                rule = jnp.where(
                    (lag == 0) | (lag == 1) | ((extra == 1) & (lag > 0)), jnp.int32(1), jnp.int32(0)
                )
                if part:
                    rule = rule * half
                allowed = jnp.where(lane_block == query_block, rule, allowed)
            caps = jnp.where(allowed == 1, pos_big, neg_big)
            if not part:
                caps = jnp.where(row + key_block * block_len <= lane, caps, neg_big)
            first = part * rows_here + key_block * block_len
            caps_ref[first : first + block_len, :] = caps
    slots = usable_ref.shape[0]
    per_group = (caps_ref.shape[0] - 2 * rows_here) // slots
    for slot in range(slots):
        first = 2 * rows_here + slot * per_group
        caps_ref[first : first + per_group, :] = jnp.full(
            (per_group, rows_here), jnp.where(usable_ref[slot] == 1, pos_big, neg_big), jnp.float32
        )


def caps_call(half, usable, extra_map, rows_here, per_group):
    keys = 2 * rows_here + usable.shape[0] * per_group
    smem = pl.BlockSpec(memory_space=pltpu.SMEM)
    return pl.pallas_call(
        caps_step,
        in_specs=[smem] * 3,
        out_shape=jax.ShapeDtypeStruct((keys, rows_here), jnp.float32),
        compiler_params=pltpu.CompilerParams(vmem_limit_bytes=VMEM_GRANT),
    )(half[None], usable, extra_map)


def summary_slots(group_id, stages):
    d_core = jnp.arange(2, dtype=jnp.int32)[:, None, None]
    d_side = jnp.arange(2, dtype=jnp.int32)[None, :, None]
    level = group_id // 4 - jnp.arange(stages, dtype=jnp.int32)[None, None, :]
    side = (group_id // 2 + d_side) % 2
    owner = level * 4 + side * 2 + (group_id + d_core) % 2
    return ((level >= 0) & (owner < group_id)).astype(jnp.int32).reshape(-1)


def attention_step(
    summ_parts,
    caps_ref,
    query_ref,
    key_ref,
    val_ref,
    grad_ref,
    lower_ref,
    *rest,
):
    attn_ref, query_grad_ref, local_ref, back_ref, *summ_grad_refs, mark_ref = rest[-7:]
    mark_ref[...] = jnp.zeros(mark_ref.shape, mark_ref.dtype)
    rows_here, width = query_ref.shape
    part_slots, _, per_group, _ = rest[0].shape
    part_rows = part_slots * per_group
    half_slots = summ_parts * part_slots // 2
    half_rows = half_slots * per_group

    def summary(kind, cols):
        return [ref[:, kind, :, cols].reshape(part_rows, HD) for ref in rest[:summ_parts]]

    factor = HD ** (-0.5)
    parts = range(width // HD)
    queries, grads, keys, vals, raws, prob_grads = [], [], [], [], [], []
    for part in parts:
        cols = slice(part * HD, (part + 1) * HD)
        queries.append(query_ref[:, cols])
        grads.append(grad_ref[:, cols])
        for kind, (own_ref, into) in enumerate(((key_ref, keys), (val_ref, vals))):
            into.append(
                jnp.concatenate(
                    [
                        own_ref[:, cols],
                        lower_ref[kind, :, cols],
                        *summary(kind, cols),
                    ],
                    axis=0,
                )
            )
        raws.append(
            lax.dot_general(
                keys[part],
                queries[part],
                (((1,), (1,)), ((), ())),
                preferred_element_type=jnp.float32,
            )
        )
        prob_grads.append(
            lax.dot_general(
                vals[part], grads[part], (((1,), (1,)), ((), ())), preferred_element_type=jnp.float32
            )
        )
    for part in parts:
        cols = slice(part * HD, (part + 1) * HD)
        query, grad = queries[part], grads[part]
        raw = jnp.minimum(raws[part], caps_ref[...])
        peak = jnp.max(raw, axis=0, keepdims=True)
        grown = jnp.exp2((raw - peak) * (factor * math.log2(math.e)))
        probs = grown * (1.0 / jnp.sum(grown, axis=0, keepdims=True))
        weights = probs.astype(jnp.bfloat16)
        attn = lax.dot_general(
            vals[part], weights, (((0,), (0,)), ((), ())), preferred_element_type=jnp.float32
        ).astype(jnp.bfloat16)
        attn_ref[:, cols] = attn.T
        row_dot = jnp.sum(probs * prob_grads[part], axis=0, keepdims=True)
        score_grads = (probs * (prob_grads[part] - row_dot)).astype(jnp.bfloat16)
        query_grad = lax.dot_general(
            keys[part], score_grads, (((0,), (0,)), ((), ())), preferred_element_type=jnp.float32
        )
        query_grad_ref[:, cols] = (query_grad * factor).astype(jnp.bfloat16).T
        key_terms = (
            jnp.dot(score_grads, query, preferred_element_type=jnp.float32) * factor
        ).astype(jnp.bfloat16)
        val_terms = jnp.dot(weights, grad, preferred_element_type=jnp.float32).astype(
            jnp.bfloat16
        )
        for kind, terms in enumerate((key_terms, val_terms)):
            local_ref[kind, :, cols] = terms[:rows_here]
            back_ref[kind, :, cols] = terms[rows_here : 2 * rows_here]
            first = 2 * rows_here
            for i, ref in enumerate(summ_grad_refs):
                begin = first + i * half_rows
                ref[:, kind, :, cols] = terms[begin : begin + half_rows].reshape(
                    half_slots, per_group, HD
                )


def attention_call(
    caps,
    full,
    lower,
    width,
    lower_col,
    summaries,
    first_col,
    summ_col,
    wide_done,
    round_width,
    round_col,
    round_done,
    after,
    effort,
):
    rows_here, total_width = full[0].shape
    tile = math.gcd(width, 2 * HD)
    slots, _, per_group, _ = summaries[0].shape
    half_slots = len(summaries) * slots // 2
    first = first_col // tile
    summ_first = summ_col // tile
    lower_first = lower_col // tile
    round_first = round_col // tile
    wide_spec = pl.BlockSpec((rows_here, tile), lambda i: (0, first + i))
    pair_spec = pl.BlockSpec((2, rows_here, tile), lambda i: (0, 0, i))
    summ_in = pl.BlockSpec((slots, 2, per_group, tile), lambda i: (0, 0, 0, summ_first + i))
    summ_out = pl.BlockSpec(
        (half_slots, 2, per_group, tile), lambda i: (0, 0, 0, round_first + i)
    )
    wide = jax.ShapeDtypeStruct((rows_here, total_width), jnp.bfloat16)
    pair = jax.ShapeDtypeStruct((2, rows_here, width), jnp.bfloat16)
    wide_pair = jax.ShapeDtypeStruct((2, rows_here, total_width), jnp.bfloat16)
    wide_pair_spec = pl.BlockSpec((2, rows_here, tile), lambda i: (0, 0, first + i))
    summ = jax.ShapeDtypeStruct((half_slots, 2, per_group, round_width), jnp.bfloat16)
    mark = jax.ShapeDtypeStruct((per_group, 5 * total_width // 8), jnp.bfloat16)
    keys = caps.shape[0]
    heads = width // HD
    ahead = 6 + len(summaries)
    aliases = {ahead + i: i for i in range(len(wide_done))}
    aliases.update({ahead + len(wide_done) + i: 4 + i for i in range(len(round_done))})
    return pl.pallas_call(
        functools.partial(attention_step, len(summaries)),
        grid=(width // tile,),
        in_specs=[pl.BlockSpec(caps.shape, lambda i: (0, 0))]
        + [wide_spec] * 4
        + [pl.BlockSpec((2, rows_here, tile), lambda i: (0, 0, lower_first + i))]
        + [summ_in] * len(summaries)
        + [pl.BlockSpec(memory_space=pl.ANY)] * (len(aliases) + len(after)),
        out_specs=[
            wide_spec,
            wide_spec,
            wide_pair_spec,
            pair_spec,
            summ_out,
            summ_out,
            pl.BlockSpec(mark.shape, lambda i: (0, 0)),
        ],
        out_shape=[wide, wide, wide_pair, pair, summ, summ, mark],
        input_output_aliases=aliases,
        compiler_params=pltpu.CompilerParams(vmem_limit_bytes=VMEM_GRANT),
        cost_estimate=pl.CostEstimate(
            flops=effort * heads * keys * rows_here * HD,
            bytes_accessed=heads * 16 * 2 * rows_here * HD,
            transcendentals=heads * keys * rows_here,
        ),
    )(caps, *full, lower, *summaries, *wide_done, *round_done, *after)


def merge_step(bounds, local_ref, *refs):
    outs = refs[-2:]
    step = pl.program_id(0)
    for part in range(len(bounds) - 1):

        @pl.when((step >= bounds[part]) & (step < bounds[part + 1]))
        def _():
            for kind, out_ref in enumerate(outs):
                total = local_ref[kind].astype(jnp.float32) + refs[part][kind].astype(jnp.float32)
                out_ref[...] = total.astype(jnp.bfloat16)


def merge_call(local, backs, first_col, carried):
    _, rows_here, total_width = local.shape
    tile = functools.reduce(math.gcd, [part.shape[2] for part in backs], 4 * HD)
    first = first_col // tile
    bounds = [sum(part.shape[2] for part in backs[:i]) // tile for i in range(len(backs) + 1)]

    def part_spec(part):
        low, high = bounds[part], bounds[part + 1]
        return pl.BlockSpec(
            (2, rows_here, tile), lambda i: (0, 0, jnp.clip(i - low, 0, high - low - 1))
        )

    wide_spec = pl.BlockSpec((rows_here, tile), lambda i: (0, first + i))
    wide = jax.ShapeDtypeStruct((rows_here, total_width), jnp.bfloat16)
    return pl.pallas_call(
        functools.partial(merge_step, bounds),
        grid=(bounds[-1],),
        in_specs=[pl.BlockSpec((2, rows_here, tile), lambda i: (0, 0, first + i))]
        + [part_spec(part) for part in range(len(backs))]
        + [pl.BlockSpec(memory_space=pl.ANY)] * len(carried),
        out_specs=[wide_spec, wide_spec],
        out_shape=[wide, wide],
        input_output_aliases={1 + len(backs) + i: i for i in range(len(carried))},
        compiler_params=pltpu.CompilerParams(vmem_limit_bytes=VMEM_GRANT),
        cost_estimate=pl.CostEstimate(
            flops=2 * rows_here * tile * bounds[-1],
            bytes_accessed=12 * rows_here * tile * bounds[-1],
            transcendentals=0,
        ),
    )(local, *backs, *carried)


def place_step(rows_ref, summ_ref, key_ref, val_ref, key_out_ref, val_out_ref, tiles, sems):
    _, few, tile, _ = tiles.shape

    def copies(refs, back):
        for kind, ref in enumerate(refs):
            for step in range(few):
                first = pl.multiple_of(rows_ref[step] // tile * tile, tile)
                there = ref.at[pl.ds(first, tile), :]
                here = tiles.at[kind, step]
                yield pltpu.make_async_copy(
                    here if back else there, there if back else here, sems.at[kind, step]
                )

    for copy in copies((key_ref, val_ref), False):
        copy.start()
    for copy in copies((key_ref, val_ref), False):
        copy.wait()
    row = lax.broadcasted_iota(jnp.int32, (tile, few), 0)
    slot = lax.broadcasted_iota(jnp.int32, (tile, few), 1)
    for step in range(few):
        place = lax.rem(rows_ref[step], tile)
        spread = jnp.where((row == place) & (slot == step), 1.0, 0.0).astype(jnp.bfloat16)
        for kind in range(2):
            moved = jnp.dot(spread, summ_ref[kind], preferred_element_type=jnp.float32)
            total = tiles[kind, step].astype(jnp.float32) + moved
            tiles[kind, step] = total.astype(jnp.bfloat16)
    for copy in copies((key_out_ref, val_out_ref), True):
        copy.start()
    for copy in copies((key_out_ref, val_out_ref), True):
        copy.wait()


def place_call(rows, summ, key_grad, val_grad):
    _, few, total_width = summ.shape
    any_spec = pl.BlockSpec(memory_space=pl.ANY)
    wide = jax.ShapeDtypeStruct(key_grad.shape, key_grad.dtype)
    return pl.pallas_call(
        place_step,
        in_specs=[
            pl.BlockSpec(memory_space=pltpu.SMEM),
            pl.BlockSpec(memory_space=pltpu.VMEM),
            any_spec,
            any_spec,
        ],
        out_specs=[any_spec, any_spec],
        out_shape=[wide, wide],
        scratch_shapes=[
            pltpu.VMEM((2, few, 16, total_width), jnp.bfloat16),
            pltpu.SemaphoreType.DMA((2, few)),
        ],
        input_output_aliases={2: 0, 3: 1},
        compiler_params=pltpu.CompilerParams(vmem_limit_bytes=VMEM_GRANT),
        cost_estimate=pl.CostEstimate(
            flops=64 * few * few * total_width,
            bytes_accessed=128 * few * total_width,
            transcendentals=0,
        ),
    )(rows, summ, key_grad, val_grad)


def pick_step(place_ref, rows_ref, key_ref, val_ref, out_ref, tiles, sems):
    _, few, tile, _ = tiles.shape
    rows_here = key_ref.shape[0]
    half = place_ref[0]

    def here(step):
        return rows_ref[0, half * few + step] - half * rows_here

    def copies():
        for kind, ref in enumerate((key_ref, val_ref)):
            for step in range(few):
                first = pl.multiple_of(here(step) // tile * tile, tile)
                yield pltpu.make_async_copy(
                    ref.at[pl.ds(first, tile), :], tiles.at[kind, step], sems.at[kind, step]
                )

    for copy in copies():
        copy.start()
    for copy in copies():
        copy.wait()
    row = lax.broadcasted_iota(jnp.int32, (few, tile), 0)
    lane = lax.broadcasted_iota(jnp.int32, (few, tile), 1)
    for kind in range(2):
        rows = jnp.zeros(out_ref.shape[1:], jnp.float32)
        for step in range(few):
            hit = (row == step) & (lane == lax.rem(here(step), tile))
            picker = jnp.where(hit, 1.0, 0.0).astype(jnp.bfloat16)
            rows = rows + jnp.dot(picker, tiles[kind, step], preferred_element_type=jnp.float32)
        out_ref[kind] = rows.astype(jnp.bfloat16)


def pick_call(half, summary_rows, key_vectors, value_vectors):
    total_width = key_vectors.shape[1]
    few = summary_rows.shape[1] // 2
    any_spec = pl.BlockSpec(memory_space=pl.ANY)
    smem = pl.BlockSpec(memory_space=pltpu.SMEM)
    return pl.pallas_call(
        pick_step,
        in_specs=[smem, smem, any_spec, any_spec],
        out_shape=jax.ShapeDtypeStruct((2, few, total_width), jnp.bfloat16),
        scratch_shapes=[
            pltpu.VMEM((2, few, 16, total_width), jnp.bfloat16),
            pltpu.SemaphoreType.DMA((2, few)),
        ],
        compiler_params=pltpu.CompilerParams(vmem_limit_bytes=VMEM_GRANT),
    )(half[None], summary_rows, key_vectors, value_vectors)


def wait_for(array, mark):
    return array + mark[:, : array.shape[-1]]


def wait_for_moved(array, moved):
    return array + jnp.minimum(jnp.abs(moved[0, :1, :1]), 0)


def add_rounded(*terms):
    total = terms[0].astype(jnp.float32)
    for term in terms[1:]:
        total = total + term.astype(jnp.float32)
    return total.astype(jnp.bfloat16)


def token_split(queries, key_vectors, value_vectors, out_grads, extra_blocks, summary_rows):
    rows_here, total_width = queries.shape
    seq_count = lax.axis_size("seq")
    stages = seq_count // 4
    group_id = lax.axis_index("seq")
    half = lax.axis_index("head")
    per_group = summary_rows.shape[1]
    few = per_group // 2
    flip_core = [(i, i ^ 1) for i in range(seq_count)]
    flip_side = [(i, i ^ 2) for i in range(seq_count)]
    flip_half = [(0, 1), (1, 0)]

    def climb(step):
        return [(i, i + 4 * step) for i in range(seq_count - 4 * step)]

    def descend(step):
        return [(i + 4 * step, i) for i in range(seq_count - 4 * step)]

    unit = total_width // 8
    chunks = [1, 2, 3, 2]
    gather_starts = [0, 2]
    edges = [sum(chunks[:i]) for i in range(len(chunks) + 1)]

    mine = pick_call(half, summary_rows, key_vectors, value_vectors)
    other = lax.ppermute(mine, "head", flip_half)

    def lower_pair(first, last, zeros=None):
        cols = slice(edges[first] * unit, edges[last] * unit)
        pair = jnp.stack([key_vectors[:, cols], value_vectors[:, cols]])
        if zeros is not None:
            pair = pair + zeros[:1, : pair.shape[2]]
        lowers.append(lax.ppermute(pair, "head", [(0, 1)]))
        lower_starts.append(first)

    both = jnp.concatenate([mine, other], axis=1)

    def span(first, last):
        return slice(edges[first] * unit, edges[last] * unit)

    def climb_stages(first, last, before=None):
        ladder = both[:, :, span(first, last)][None]
        if before is not None:
            ladder = ladder + jnp.minimum(jnp.abs(before[1, :1, :1, :1]), 0)
        return jnp.concatenate(
            [ladder] + [lax.ppermute(ladder, "seq", climb(i)) for i in range(1, stages)], axis=0
        )

    def with_other_core(near):
        return near, lax.ppermute(near, "seq", flip_core)

    def reduce_chip(near_grad, far_grad):
        return add_rounded(near_grad, lax.ppermute(far_grad, "seq", flip_core))

    def reduce_plane(chip):
        return add_rounded(chip[:stages], lax.ppermute(chip[stages:], "seq", flip_side))

    def reduce_group(plane):
        return add_rounded(
            plane[0],
            *[lax.ppermute(plane[i], "seq", descend(i)) for i in range(1, stages)],
        )

    def reduce_group_halving(plane):
        while plane.shape[0] > 1 and plane.shape[0] % 2 == 0:
            size = plane.shape[0] // 2
            plane = add_rounded(plane[:size], lax.ppermute(plane[size:], "seq", descend(size)))
        return reduce_group(plane) if plane.shape[0] > 1 else plane[0]

    def reduce_half(groups):
        group = jnp.concatenate(groups, axis=2)
        return add_rounded(group[:, :few], lax.ppermute(group[:, few:], "head", flip_half))

    usable = summary_slots(group_id, stages)
    caps = caps_call(half, usable, extra_blocks[0], rows_here, per_group)
    full = (queries, key_vectors, value_vectors, out_grads)

    lowers = []
    lower_starts = []
    gathered = []
    marks = []
    wide_done = ()
    backs = []

    def attend(chunk, source, reduce_first, reduce_last, round_done, after, effort=56):
        nonlocal wide_done
        low = max(start for start in lower_starts if start <= chunk)
        out = attention_call(
            caps,
            full,
            lowers[lower_starts.index(low)],
            (edges[chunk + 1] - edges[chunk]) * unit,
            (edges[chunk] - edges[low]) * unit,
            gathered[source],
            edges[chunk] * unit,
            (edges[chunk] - edges[gather_starts[source]]) * unit,
            wide_done,
            (edges[reduce_last] - edges[reduce_first]) * unit,
            (edges[chunk] - edges[reduce_first]) * unit,
            round_done,
            after,
            effort,
        )
        wide_done = tuple(out[:3])
        backs.append(lax.ppermute(out[3], "head", [(1, 0)]))
        marks.append(out[-1])
        return tuple(out[4:-1])

    rows_mine = lax.dynamic_slice_in_dim(summary_rows[0], half * few, few, 0) - half * rows_here

    lower_pair(0, 2)
    ladder = climb_stages(0, 2)
    first_ladder = ladder
    side = lax.ppermute(ladder, "seq", flip_side)
    lower_pair(2, 3, jnp.minimum(jnp.abs(side[0, 0]), 0))
    gathered.append(with_other_core(jnp.concatenate([ladder, side], axis=0)))
    ladder = climb_stages(2, 4, first_ladder)
    done = attend(0, 0, 0, 2, (), ())
    ladder = wait_for(ladder, marks[0])
    side = lax.ppermute(ladder, "seq", flip_side)
    done = attend(1, 0, 0, 2, done, ())
    near = wait_for(jnp.concatenate([ladder, side], axis=0), marks[1])
    near = wait_for_moved(near, backs[0])
    gathered.append(with_other_core(near))
    lower_pair(3, 4, jnp.minimum(jnp.abs(near[0, 0]), 0))
    chip_a = reduce_chip(*done)
    done = attend(2, 1, 2, 3, (), (), 16)
    chip_a = wait_for(chip_a, marks[2])
    plane_a = reduce_plane(chip_a)
    chip_b = reduce_chip(*done)
    done = attend(3, 1, 3, 4, (), (backs[1], chip_a))
    chip_b = wait_for(chip_b, marks[3])
    plane_b = reduce_plane(chip_b)
    chip_c = wait_for_moved(reduce_chip(*done), backs[2])
    plane_c = reduce_plane(chip_c)
    group_a = reduce_group_halving(plane_a)
    merged = merge_call(wide_done[2], backs[:3], 0, ())
    plane_b = wait_for_moved(jnp.concatenate([plane_b, plane_c], axis=3), merged[0][None])
    group_b = wait_for_moved(reduce_group(plane_b), backs[3])
    merged = merge_call(wide_done[2], backs[3:], edges[3] * unit, tuple(merged))
    finished = place_call(rows_mine, reduce_half([group_a, group_b]), *merged)
    return (*wide_done[:2], *finished)


def solution(mesh):
    placed = (
        P(("seq", "head"), None),
        P(("seq", "head"), None),
        P(("seq", "head"), None),
        P(("seq", "head"), None),
        P("seq", None, None),
        P("seq", None),
    )
    paired = mesh.shape["head"] == 2 and mesh.shape["seq"] % 4 == 0
    return jax.shard_map(
        token_split if paired else per_device,
        mesh=mesh,
        in_specs=placed,
        out_specs=(
            P(("seq", "head"), None),
            P(("seq", "head"), None),
            P(("seq", "head"), None),
            P(("seq", "head"), None),
        ),
        check_vma=False,
    )
```

```python
import functools
import math

import jax
import jax.numpy as jnp
from jax import lax
from jax.experimental import pallas as pl
from jax.experimental.pallas import tpu as pltpu
from jax.sharding import PartitionSpec as P

HD = 128


neg_big = -1e30
pos_big = 3.4028235e38


def head_scores(query_heads, key_heads, factor):
    return (
        jnp.einsum("qhd,khd->hqk", query_heads, key_heads, preferred_element_type=jnp.float32)
        * factor
    )


def local_allowed(extra_map, group_len):
    block_count = extra_map.shape[0]
    block_len = group_len // block_count
    block_ids = jnp.arange(block_count, dtype=jnp.int32)
    block_lag = block_ids[:, None] - block_ids[None, :]
    allowed = (block_lag == 0) | (block_lag == 1) | (extra_map == 1) & (block_lag > 0)
    allowed = jnp.repeat(jnp.repeat(allowed, block_len, axis=0), block_len, axis=1)
    positions = jnp.arange(group_len, dtype=jnp.int32)
    return allowed & (positions[None, :] <= positions[:, None])


def key_window(summary_keys, summary_vals, block_id, key_rows, lower_end, upper_end, per_group):
    offset = block_id * key_rows
    key_block = lax.dynamic_slice_in_dim(summary_keys, offset, key_rows, 0)
    val_block = lax.dynamic_slice_in_dim(summary_vals, offset, key_rows, 0)
    owners = (offset + jnp.arange(key_rows, dtype=jnp.int32)) // per_group
    usable = (owners >= lower_end) & (owners < upper_end)
    return (offset, key_block, val_block, usable[None, None, :])


def block_bounds(lower_end, upper_end, key_rows, per_group):
    begin_block = lower_end * per_group // key_rows
    end_block = (upper_end * per_group + key_rows - 1) // key_rows
    return (begin_block, jnp.where(upper_end > lower_end, end_block, begin_block))


def softmax_stats(
    query_heads, summary_keys, summary_vals, lower_end, upper_end, key_rows, per_group, factor
):
    begin_block, end_block = block_bounds(lower_end, upper_end, key_rows, per_group)

    def softmax_advance(block_id, carried):
        peak, summed = carried
        offset, key_block, val_block, usable = key_window(
            summary_keys, summary_vals, block_id, key_rows, lower_end, upper_end, per_group
        )
        scores = jnp.where(usable, head_scores(query_heads, key_block, factor), neg_big)
        new_peak = jnp.maximum(peak, jnp.max(scores, axis=2))
        summed = summed * jnp.exp(peak - new_peak) + jnp.sum(
            jnp.exp(scores - new_peak[..., None]), axis=2
        )
        return (new_peak, summed)

    shape_hq = (query_heads.shape[1], query_heads.shape[0])
    start_stats = (jnp.full(shape_hq, neg_big, jnp.float32), jnp.zeros(shape_hq, jnp.float32))
    return lax.fori_loop(begin_block, end_block, softmax_advance, start_stats)


def merge_stats(earlier, later):
    peak = jnp.maximum(earlier[0], later[0])
    return (peak, earlier[1] * jnp.exp(earlier[0] - peak) + later[1] * jnp.exp(later[0] - peak))


def weighted_values(
    query_heads,
    log_mass,
    summary_keys,
    summary_vals,
    lower_end,
    upper_end,
    key_rows,
    per_group,
    factor,
):
    begin_block, end_block = block_bounds(lower_end, upper_end, key_rows, per_group)

    def weighted_advance(block_id, summed_values):
        offset, key_block, val_block, usable = key_window(
            summary_keys, summary_vals, block_id, key_rows, lower_end, upper_end, per_group
        )
        weights = jnp.where(
            usable, jnp.exp(head_scores(query_heads, key_block, factor) - log_mass[..., None]), 0.0
        ).astype(jnp.bfloat16)
        return summed_values + jnp.einsum(
            "hqk,khd->qhd", weights, val_block, preferred_element_type=jnp.float32
        )

    return lax.fori_loop(
        begin_block, end_block, weighted_advance, jnp.zeros(query_heads.shape, jnp.float32)
    )


def summary_backward(
    query_heads,
    grad_heads,
    log_mass,
    row_dot,
    summary_keys,
    summary_vals,
    lower_end,
    upper_end,
    key_rows,
    per_group,
    factor,
    carried,
):
    begin_block, end_block = block_bounds(lower_end, upper_end, key_rows, per_group)

    def summary_advance(block_id, running):
        query_acc, key_terms, val_terms = running
        offset, key_block, val_block, usable = key_window(
            summary_keys, summary_vals, block_id, key_rows, lower_end, upper_end, per_group
        )
        attn_probs = jnp.where(
            usable, jnp.exp(head_scores(query_heads, key_block, factor) - log_mass[..., None]), 0.0
        )
        weights = attn_probs.astype(jnp.bfloat16)
        prob_grads = jnp.einsum(
            "qhd,khd->hqk", grad_heads, val_block, preferred_element_type=jnp.float32
        )
        score_grads = (attn_probs * (prob_grads - row_dot[..., None])).astype(jnp.bfloat16)
        query_acc = (
            query_acc
            + jnp.einsum("hqk,khd->qhd", score_grads, key_block, preferred_element_type=jnp.float32)
            * factor
        )
        key_part = (
            jnp.einsum("hqk,qhd->khd", score_grads, query_heads, preferred_element_type=jnp.float32)
            * factor
        )
        val_part = jnp.einsum(
            "hqk,qhd->khd", weights, grad_heads, preferred_element_type=jnp.float32
        )
        key_terms = lax.dynamic_update_slice_in_dim(
            key_terms,
            lax.dynamic_slice_in_dim(key_terms, offset, key_rows, 0) + key_part,
            offset,
            0,
        )
        val_terms = lax.dynamic_update_slice_in_dim(
            val_terms,
            lax.dynamic_slice_in_dim(val_terms, offset, key_rows, 0) + val_part,
            offset,
            0,
        )
        return (query_acc, key_terms, val_terms)

    return lax.fori_loop(begin_block, end_block, summary_advance, carried)


def per_device(queries, key_vectors, value_vectors, out_grads, extra_blocks, summary_rows):
    query_all, key_all, val_all, grad_all = (
        lax.all_to_all(queries, "head", split_axis=1, concat_axis=0, tiled=True),
        lax.all_to_all(key_vectors, "head", split_axis=1, concat_axis=0, tiled=True),
        lax.all_to_all(value_vectors, "head", split_axis=1, concat_axis=0, tiled=True),
        lax.all_to_all(out_grads, "head", split_axis=1, concat_axis=0, tiled=True),
    )
    group_len, local_width = query_all.shape
    head_count = local_width // HD
    factor = HD ** (-0.5)
    query_heads = query_all.reshape(group_len, head_count, HD)
    key_heads = key_all.reshape(group_len, head_count, HD)
    val_heads = val_all.reshape(group_len, head_count, HD)
    grad_heads = grad_all.reshape(group_len, head_count, HD)
    per_group = summary_rows.shape[1]
    seq_count = lax.axis_size("seq")
    group_id = lax.axis_index("seq")
    picker = summary_rows[0][:, None] == jnp.arange(group_len, dtype=jnp.int32)[None, :]
    own_keys = jnp.dot(
        picker.astype(jnp.bfloat16), key_all, preferred_element_type=jnp.float32
    ).astype(jnp.bfloat16)
    own_vals = jnp.dot(
        picker.astype(jnp.bfloat16), val_all, preferred_element_type=jnp.float32
    ).astype(jnp.bfloat16)
    summ_keys_flat, summ_vals_flat = (
        lax.all_gather(own_keys, "seq", axis=0, tiled=True),
        lax.all_gather(own_vals, "seq", axis=0, tiled=True),
    )
    total_rows = summ_keys_flat.shape[0]
    summary_keys = summ_keys_flat.reshape(total_rows, head_count, HD)
    summary_vals = summ_vals_flat.reshape(total_rows, head_count, HD)
    key_rows = per_group * math.gcd(seq_count, max(1, 128 // per_group))
    allowed = local_allowed(extra_blocks[0], group_len)
    local_scores = jnp.where(allowed[None], head_scores(query_heads, key_heads, factor), neg_big)
    local_peak = jnp.max(local_scores, axis=2)
    local_stats = (local_peak, jnp.sum(jnp.exp(local_scores - local_peak[..., None]), axis=2))
    all_stats = merge_stats(
        local_stats,
        softmax_stats(
            query_heads, summary_keys, summary_vals, 0, group_id, key_rows, per_group, factor
        ),
    )
    log_mass = all_stats[0] + jnp.log(all_stats[1])
    summ_values = weighted_values(
        query_heads, log_mass, summary_keys, summary_vals, 0, group_id, key_rows, per_group, factor
    )
    local_probs = jnp.exp(local_scores - log_mass[..., None])
    local_weights = local_probs.astype(jnp.bfloat16)
    attention = (
        summ_values
        + jnp.einsum("hqk,khd->qhd", local_weights, val_heads, preferred_element_type=jnp.float32)
    ).astype(jnp.bfloat16)
    row_dot = jnp.einsum("qhd,qhd->hq", grad_heads, attention, preferred_element_type=jnp.float32)
    local_prob_grads = jnp.einsum(
        "qhd,khd->hqk", grad_heads, val_heads, preferred_element_type=jnp.float32
    )
    local_score_grads = (local_probs * (local_prob_grads - row_dot[..., None])).astype(jnp.bfloat16)
    query_local = (
        jnp.einsum("hqk,khd->qhd", local_score_grads, key_heads, preferred_element_type=jnp.float32)
        * factor
    )
    key_local = (
        jnp.einsum(
            "hqk,qhd->khd", local_score_grads, query_heads, preferred_element_type=jnp.float32
        )
        * factor
    )
    val_local = jnp.einsum(
        "hqk,qhd->khd", local_weights, grad_heads, preferred_element_type=jnp.float32
    )
    empty_terms = jnp.zeros((total_rows, head_count, HD), jnp.float32)
    start_running = (jnp.zeros(query_heads.shape, jnp.float32), empty_terms, empty_terms)
    query_summ, key_terms, val_terms = summary_backward(
        query_heads,
        grad_heads,
        log_mass,
        row_dot,
        summary_keys,
        summary_vals,
        0,
        group_id,
        key_rows,
        per_group,
        factor,
        start_running,
    )
    recv_keys, recv_vals = (
        lax.all_to_all(
            key_terms.astype(jnp.bfloat16), "seq", split_axis=0, concat_axis=0, tiled=True
        ).astype(key_terms.dtype),
        lax.all_to_all(
            val_terms.astype(jnp.bfloat16), "seq", split_axis=0, concat_axis=0, tiled=True
        ).astype(val_terms.dtype),
    )
    summ_key_grad = jnp.sum(recv_keys.reshape(seq_count, per_group, head_count, HD), axis=0)
    summ_val_grad = jnp.sum(recv_vals.reshape(seq_count, per_group, head_count, HD), axis=0)
    picker_f = picker.astype(jnp.float32)
    key_grad = key_local + jnp.einsum(
        "sq,shd->qhd", picker_f, summ_key_grad, precision=lax.Precision.HIGHEST
    )
    value_grad = val_local + jnp.einsum(
        "sq,shd->qhd", picker_f, summ_val_grad, precision=lax.Precision.HIGHEST
    )
    query_grad = query_local + query_summ
    outputs = (
        attention.reshape(group_len, local_width),
        query_grad.astype(jnp.bfloat16).reshape(group_len, local_width),
        key_grad.astype(jnp.bfloat16).reshape(group_len, local_width),
        value_grad.astype(jnp.bfloat16).reshape(group_len, local_width),
    )
    attention_out, query_out, key_out, value_out = (
        lax.all_to_all(outputs[0], "head", split_axis=0, concat_axis=1, tiled=True),
        lax.all_to_all(outputs[1], "head", split_axis=0, concat_axis=1, tiled=True),
        lax.all_to_all(outputs[2], "head", split_axis=0, concat_axis=1, tiled=True),
        lax.all_to_all(outputs[3], "head", split_axis=0, concat_axis=1, tiled=True),
    )
    return (attention_out, query_out, key_out, value_out)


VMEM_GRANT = 60 * 1024 * 1024


def caps_step(place_ref, usable_ref, extra_ref, caps_ref):
    rows_here = caps_ref.shape[1]
    mine = extra_ref.shape[0] // 2
    block_len = rows_here // mine
    half = place_ref[0]
    lane = lax.broadcasted_iota(jnp.int32, (block_len, rows_here), 1)
    row = lax.broadcasted_iota(jnp.int32, (block_len, rows_here), 0)
    lane_block = lane // block_len
    for part in range(2):
        for key_block in range(mine):
            group_block = key_block if part else half * mine + key_block
            allowed = jnp.zeros((block_len, rows_here), jnp.int32)
            for query_block in range(mine):
                lag = half * mine + query_block - group_block
                extra = extra_ref[half * mine + query_block, group_block]
                rule = jnp.where(
                    (lag == 0) | (lag == 1) | ((extra == 1) & (lag > 0)), jnp.int32(1), jnp.int32(0)
                )
                if part:
                    rule = rule * half
                allowed = jnp.where(lane_block == query_block, rule, allowed)
            caps = jnp.where(allowed == 1, pos_big, neg_big)
            if not part:
                caps = jnp.where(row + key_block * block_len <= lane, caps, neg_big)
            first = part * rows_here + key_block * block_len
            caps_ref[first : first + block_len, :] = caps
    slots = usable_ref.shape[0]
    per_group = (caps_ref.shape[0] - 2 * rows_here) // slots
    for slot in range(slots):
        first = 2 * rows_here + slot * per_group
        caps_ref[first : first + per_group, :] = jnp.full(
            (per_group, rows_here), jnp.where(usable_ref[slot] == 1, pos_big, neg_big), jnp.float32
        )


def caps_call(half, usable, extra_map, rows_here, per_group):
    keys = 2 * rows_here + usable.shape[0] * per_group
    smem = pl.BlockSpec(memory_space=pltpu.SMEM)
    return pl.pallas_call(
        caps_step,
        in_specs=[smem] * 3,
        out_shape=jax.ShapeDtypeStruct((keys, rows_here), jnp.float32),
        compiler_params=pltpu.CompilerParams(vmem_limit_bytes=VMEM_GRANT),
    )(half[None], usable, extra_map)


def summary_slots(group_id, stages):
    d_core = jnp.arange(2, dtype=jnp.int32)[:, None, None]
    d_side = jnp.arange(2, dtype=jnp.int32)[None, :, None]
    level = group_id // 4 - jnp.arange(stages, dtype=jnp.int32)[None, None, :]
    side = (group_id // 2 + d_side) % 2
    owner = level * 4 + side * 2 + (group_id + d_core) % 2
    return ((level >= 0) & (owner < group_id)).astype(jnp.int32).reshape(-1)


def attention_step(
    summ_parts,
    caps_ref,
    query_ref,
    key_ref,
    val_ref,
    grad_ref,
    lower_ref,
    *rest,
):
    attn_ref, query_grad_ref, local_ref, back_ref, *summ_grad_refs, mark_ref = rest[-7:]
    mark_ref[...] = jnp.zeros(mark_ref.shape, mark_ref.dtype)
    rows_here, width = query_ref.shape
    part_slots, _, per_group, _ = rest[0].shape
    part_rows = part_slots * per_group
    half_slots = summ_parts * part_slots // 2
    half_rows = half_slots * per_group

    def summary(kind, cols):
        return [ref[:, kind, :, cols].reshape(part_rows, HD) for ref in rest[:summ_parts]]

    factor = HD ** (-0.5)
    parts = range(width // HD)
    queries, grads, keys, vals, raws, prob_grads = [], [], [], [], [], []
    for part in parts:
        cols = slice(part * HD, (part + 1) * HD)
        queries.append(query_ref[:, cols])
        grads.append(grad_ref[:, cols])
        for kind, (own_ref, into) in enumerate(((key_ref, keys), (val_ref, vals))):
            into.append(
                jnp.concatenate(
                    [
                        own_ref[:, cols],
                        lower_ref[kind, :, cols],
                        *summary(kind, cols),
                    ],
                    axis=0,
                )
            )
        raws.append(
            lax.dot_general(
                keys[part],
                queries[part],
                (((1,), (1,)), ((), ())),
                preferred_element_type=jnp.float32,
            )
        )
        prob_grads.append(
            lax.dot_general(
                vals[part], grads[part], (((1,), (1,)), ((), ())), preferred_element_type=jnp.float32
            )
        )
    for part in parts:
        cols = slice(part * HD, (part + 1) * HD)
        query, grad = queries[part], grads[part]
        raw = jnp.minimum(raws[part], caps_ref[...])
        peak = jnp.max(raw, axis=0, keepdims=True)
        grown = jnp.exp2((raw - peak) * (factor * math.log2(math.e)))
        probs = grown * (1.0 / jnp.sum(grown, axis=0, keepdims=True))
        weights = probs.astype(jnp.bfloat16)
        attn = lax.dot_general(
            vals[part], weights, (((0,), (0,)), ((), ())), preferred_element_type=jnp.float32
        ).astype(jnp.bfloat16)
        attn_ref[:, cols] = attn.T
        row_dot = jnp.sum(probs * prob_grads[part], axis=0, keepdims=True)
        score_grads = (probs * (prob_grads[part] - row_dot)).astype(jnp.bfloat16)
        query_grad = lax.dot_general(
            keys[part], score_grads, (((0,), (0,)), ((), ())), preferred_element_type=jnp.float32
        )
        query_grad_ref[:, cols] = (query_grad * factor).astype(jnp.bfloat16).T
        key_terms = (
            jnp.dot(score_grads, query, preferred_element_type=jnp.float32) * factor
        ).astype(jnp.bfloat16)
        val_terms = jnp.dot(weights, grad, preferred_element_type=jnp.float32).astype(
            jnp.bfloat16
        )
        for kind, terms in enumerate((key_terms, val_terms)):
            local_ref[kind, :, cols] = terms[:rows_here]
            back_ref[kind, :, cols] = terms[rows_here : 2 * rows_here]
            first = 2 * rows_here
            for i, ref in enumerate(summ_grad_refs):
                begin = first + i * half_rows
                ref[:, kind, :, cols] = terms[begin : begin + half_rows].reshape(
                    half_slots, per_group, HD
                )


def attention_call(
    caps,
    full,
    lower,
    width,
    lower_col,
    summaries,
    first_col,
    summ_col,
    wide_done,
    round_width,
    round_col,
    round_done,
    after,
    effort,
):
    rows_here, total_width = full[0].shape
    tile = math.gcd(width, 2 * HD)
    slots, _, per_group, _ = summaries[0].shape
    half_slots = len(summaries) * slots // 2
    first = first_col // tile
    summ_first = summ_col // tile
    lower_first = lower_col // tile
    round_first = round_col // tile
    wide_spec = pl.BlockSpec((rows_here, tile), lambda i: (0, first + i))
    pair_spec = pl.BlockSpec((2, rows_here, tile), lambda i: (0, 0, i))
    summ_in = pl.BlockSpec((slots, 2, per_group, tile), lambda i: (0, 0, 0, summ_first + i))
    summ_out = pl.BlockSpec(
        (half_slots, 2, per_group, tile), lambda i: (0, 0, 0, round_first + i)
    )
    wide = jax.ShapeDtypeStruct((rows_here, total_width), jnp.bfloat16)
    pair = jax.ShapeDtypeStruct((2, rows_here, width), jnp.bfloat16)
    wide_pair = jax.ShapeDtypeStruct((2, rows_here, total_width), jnp.bfloat16)
    wide_pair_spec = pl.BlockSpec((2, rows_here, tile), lambda i: (0, 0, first + i))
    summ = jax.ShapeDtypeStruct((half_slots, 2, per_group, round_width), jnp.bfloat16)
    mark = jax.ShapeDtypeStruct((per_group, 5 * total_width // 8), jnp.bfloat16)
    keys = caps.shape[0]
    heads = width // HD
    ahead = 6 + len(summaries)
    aliases = {ahead + i: i for i in range(len(wide_done))}
    aliases.update({ahead + len(wide_done) + i: 4 + i for i in range(len(round_done))})
    return pl.pallas_call(
        functools.partial(attention_step, len(summaries)),
        grid=(width // tile,),
        in_specs=[pl.BlockSpec(caps.shape, lambda i: (0, 0))]
        + [wide_spec] * 4
        + [pl.BlockSpec((2, rows_here, tile), lambda i: (0, 0, lower_first + i))]
        + [summ_in] * len(summaries)
        + [pl.BlockSpec(memory_space=pl.ANY)] * (len(aliases) + len(after)),
        out_specs=[
            wide_spec,
            wide_spec,
            wide_pair_spec,
            pair_spec,
            summ_out,
            summ_out,
            pl.BlockSpec(mark.shape, lambda i: (0, 0)),
        ],
        out_shape=[wide, wide, wide_pair, pair, summ, summ, mark],
        input_output_aliases=aliases,
        compiler_params=pltpu.CompilerParams(vmem_limit_bytes=VMEM_GRANT),
        cost_estimate=pl.CostEstimate(
            flops=effort * heads * keys * rows_here * HD,
            bytes_accessed=heads * 16 * 2 * rows_here * HD,
            transcendentals=heads * keys * rows_here,
        ),
    )(caps, *full, lower, *summaries, *wide_done, *round_done, *after)


def merge_step(bounds, local_ref, *refs):
    outs = refs[-2:]
    step = pl.program_id(0)
    for part in range(len(bounds) - 1):

        @pl.when((step >= bounds[part]) & (step < bounds[part + 1]))
        def _():
            for kind, out_ref in enumerate(outs):
                total = local_ref[kind].astype(jnp.float32) + refs[part][kind].astype(jnp.float32)
                out_ref[...] = total.astype(jnp.bfloat16)


def merge_call(local, backs, first_col, carried):
    _, rows_here, total_width = local.shape
    tile = functools.reduce(math.gcd, [part.shape[2] for part in backs], 4 * HD)
    first = first_col // tile
    bounds = [sum(part.shape[2] for part in backs[:i]) // tile for i in range(len(backs) + 1)]

    def part_spec(part):
        low, high = bounds[part], bounds[part + 1]
        return pl.BlockSpec(
            (2, rows_here, tile), lambda i: (0, 0, jnp.clip(i - low, 0, high - low - 1))
        )

    wide_spec = pl.BlockSpec((rows_here, tile), lambda i: (0, first + i))
    wide = jax.ShapeDtypeStruct((rows_here, total_width), jnp.bfloat16)
    return pl.pallas_call(
        functools.partial(merge_step, bounds),
        grid=(bounds[-1],),
        in_specs=[pl.BlockSpec((2, rows_here, tile), lambda i: (0, 0, first + i))]
        + [part_spec(part) for part in range(len(backs))]
        + [pl.BlockSpec(memory_space=pl.ANY)] * len(carried),
        out_specs=[wide_spec, wide_spec],
        out_shape=[wide, wide],
        input_output_aliases={1 + len(backs) + i: i for i in range(len(carried))},
        compiler_params=pltpu.CompilerParams(vmem_limit_bytes=VMEM_GRANT),
        cost_estimate=pl.CostEstimate(
            flops=2 * rows_here * tile * bounds[-1],
            bytes_accessed=12 * rows_here * tile * bounds[-1],
            transcendentals=0,
        ),
    )(local, *backs, *carried)


def place_step(rows_ref, summ_ref, key_ref, val_ref, key_out_ref, val_out_ref, tiles, sems):
    _, few, tile, _ = tiles.shape

    def copies(refs, back):
        for kind, ref in enumerate(refs):
            for step in range(few):
                first = pl.multiple_of(rows_ref[step] // tile * tile, tile)
                there = ref.at[pl.ds(first, tile), :]
                here = tiles.at[kind, step]
                yield pltpu.make_async_copy(
                    here if back else there, there if back else here, sems.at[kind, step]
                )

    for copy in copies((key_ref, val_ref), False):
        copy.start()
    for copy in copies((key_ref, val_ref), False):
        copy.wait()
    row = lax.broadcasted_iota(jnp.int32, (tile, few), 0)
    slot = lax.broadcasted_iota(jnp.int32, (tile, few), 1)
    for step in range(few):
        place = lax.rem(rows_ref[step], tile)
        spread = jnp.where((row == place) & (slot == step), 1.0, 0.0).astype(jnp.bfloat16)
        for kind in range(2):
            moved = jnp.dot(spread, summ_ref[kind], preferred_element_type=jnp.float32)
            total = tiles[kind, step].astype(jnp.float32) + moved
            tiles[kind, step] = total.astype(jnp.bfloat16)
    for copy in copies((key_out_ref, val_out_ref), True):
        copy.start()
    for copy in copies((key_out_ref, val_out_ref), True):
        copy.wait()


def place_call(rows, summ, key_grad, val_grad):
    _, few, total_width = summ.shape
    any_spec = pl.BlockSpec(memory_space=pl.ANY)
    wide = jax.ShapeDtypeStruct(key_grad.shape, key_grad.dtype)
    return pl.pallas_call(
        place_step,
        in_specs=[
            pl.BlockSpec(memory_space=pltpu.SMEM),
            pl.BlockSpec(memory_space=pltpu.VMEM),
            any_spec,
            any_spec,
        ],
        out_specs=[any_spec, any_spec],
        out_shape=[wide, wide],
        scratch_shapes=[
            pltpu.VMEM((2, few, 16, total_width), jnp.bfloat16),
            pltpu.SemaphoreType.DMA((2, few)),
        ],
        input_output_aliases={2: 0, 3: 1},
        compiler_params=pltpu.CompilerParams(vmem_limit_bytes=VMEM_GRANT),
        cost_estimate=pl.CostEstimate(
            flops=64 * few * few * total_width,
            bytes_accessed=128 * few * total_width,
            transcendentals=0,
        ),
    )(rows, summ, key_grad, val_grad)


def pick_step(place_ref, rows_ref, key_ref, val_ref, out_ref, tiles, sems):
    _, few, tile, _ = tiles.shape
    rows_here = key_ref.shape[0]
    half = place_ref[0]

    def here(step):
        return rows_ref[0, half * few + step] - half * rows_here

    def copies():
        for kind, ref in enumerate((key_ref, val_ref)):
            for step in range(few):
                first = pl.multiple_of(here(step) // tile * tile, tile)
                yield pltpu.make_async_copy(
                    ref.at[pl.ds(first, tile), :], tiles.at[kind, step], sems.at[kind, step]
                )

    for copy in copies():
        copy.start()
    for copy in copies():
        copy.wait()
    row = lax.broadcasted_iota(jnp.int32, (few, tile), 0)
    lane = lax.broadcasted_iota(jnp.int32, (few, tile), 1)
    for kind in range(2):
        rows = jnp.zeros(out_ref.shape[1:], jnp.float32)
        for step in range(few):
            hit = (row == step) & (lane == lax.rem(here(step), tile))
            picker = jnp.where(hit, 1.0, 0.0).astype(jnp.bfloat16)
            rows = rows + jnp.dot(picker, tiles[kind, step], preferred_element_type=jnp.float32)
        out_ref[kind] = rows.astype(jnp.bfloat16)


def pick_call(half, summary_rows, key_vectors, value_vectors):
    total_width = key_vectors.shape[1]
    few = summary_rows.shape[1] // 2
    any_spec = pl.BlockSpec(memory_space=pl.ANY)
    smem = pl.BlockSpec(memory_space=pltpu.SMEM)
    return pl.pallas_call(
        pick_step,
        in_specs=[smem, smem, any_spec, any_spec],
        out_shape=jax.ShapeDtypeStruct((2, few, total_width), jnp.bfloat16),
        scratch_shapes=[
            pltpu.VMEM((2, few, 16, total_width), jnp.bfloat16),
            pltpu.SemaphoreType.DMA((2, few)),
        ],
        compiler_params=pltpu.CompilerParams(vmem_limit_bytes=VMEM_GRANT),
    )(half[None], summary_rows, key_vectors, value_vectors)


def wait_for(array, mark):
    return array + mark[:, : array.shape[-1]]


def wait_for_moved(array, moved):
    return array + jnp.minimum(jnp.abs(moved[0, :1, :1]), 0)


def add_rounded(*terms):
    total = terms[0].astype(jnp.float32)
    for term in terms[1:]:
        total = total + term.astype(jnp.float32)
    return total.astype(jnp.bfloat16)


def token_split(queries, key_vectors, value_vectors, out_grads, extra_blocks, summary_rows):
    rows_here, total_width = queries.shape
    seq_count = lax.axis_size("seq")
    stages = seq_count // 4
    group_id = lax.axis_index("seq")
    half = lax.axis_index("head")
    per_group = summary_rows.shape[1]
    few = per_group // 2
    flip_core = [(i, i ^ 1) for i in range(seq_count)]
    flip_side = [(i, i ^ 2) for i in range(seq_count)]
    flip_half = [(0, 1), (1, 0)]

    def climb(step):
        return [(i, i + 4 * step) for i in range(seq_count - 4 * step)]

    def descend(step):
        return [(i + 4 * step, i) for i in range(seq_count - 4 * step)]

    unit = total_width // 8
    chunks = [1, 2, 3, 2]
    gather_starts = [0, 2]
    edges = [sum(chunks[:i]) for i in range(len(chunks) + 1)]

    mine = pick_call(half, summary_rows, key_vectors, value_vectors)
    other = lax.ppermute(mine, "head", flip_half)

    def lower_pair(first, last, zeros=None):
        cols = slice(edges[first] * unit, edges[last] * unit)
        pair = jnp.stack([key_vectors[:, cols], value_vectors[:, cols]])
        if zeros is not None:
            pair = pair + zeros[:1, : pair.shape[2]]
        lowers.append(lax.ppermute(pair, "head", [(0, 1)]))
        lower_starts.append(first)

    both = jnp.concatenate([mine, other], axis=1)

    def span(first, last):
        return slice(edges[first] * unit, edges[last] * unit)

    def climb_stages(first, last, before=None):
        ladder = both[:, :, span(first, last)][None]
        if before is not None:
            ladder = ladder + jnp.minimum(jnp.abs(before[1, :1, :1, :1]), 0)
        return jnp.concatenate(
            [ladder] + [lax.ppermute(ladder, "seq", climb(i)) for i in range(1, stages)], axis=0
        )

    def with_other_core(near):
        return near, lax.ppermute(near, "seq", flip_core)

    def reduce_chip(near_grad, far_grad):
        return add_rounded(near_grad, lax.ppermute(far_grad, "seq", flip_core))

    def reduce_plane(chip):
        return add_rounded(chip[:stages], lax.ppermute(chip[stages:], "seq", flip_side))

    def reduce_group(plane):
        return add_rounded(
            plane[0],
            *[lax.ppermute(plane[i], "seq", descend(i)) for i in range(1, stages)],
        )

    def reduce_group_halving(plane):
        while plane.shape[0] > 1 and plane.shape[0] % 2 == 0:
            size = plane.shape[0] // 2
            plane = add_rounded(plane[:size], lax.ppermute(plane[size:], "seq", descend(size)))
        return reduce_group(plane) if plane.shape[0] > 1 else plane[0]

    def reduce_half(groups):
        group = jnp.concatenate(groups, axis=2)
        return add_rounded(group[:, :few], lax.ppermute(group[:, few:], "head", flip_half))

    usable = summary_slots(group_id, stages)
    caps = caps_call(half, usable, extra_blocks[0], rows_here, per_group)
    full = (queries, key_vectors, value_vectors, out_grads)

    lowers = []
    lower_starts = []
    gathered = []
    marks = []
    wide_done = ()
    backs = []

    def attend(chunk, source, reduce_first, reduce_last, round_done, after, effort=56):
        nonlocal wide_done
        low = max(start for start in lower_starts if start <= chunk)
        out = attention_call(
            caps,
            full,
            lowers[lower_starts.index(low)],
            (edges[chunk + 1] - edges[chunk]) * unit,
            (edges[chunk] - edges[low]) * unit,
            gathered[source],
            edges[chunk] * unit,
            (edges[chunk] - edges[gather_starts[source]]) * unit,
            wide_done,
            (edges[reduce_last] - edges[reduce_first]) * unit,
            (edges[chunk] - edges[reduce_first]) * unit,
            round_done,
            after,
            effort,
        )
        wide_done = tuple(out[:3])
        backs.append(lax.ppermute(out[3], "head", [(1, 0)]))
        marks.append(out[-1])
        return tuple(out[4:-1])

    rows_mine = lax.dynamic_slice_in_dim(summary_rows[0], half * few, few, 0) - half * rows_here

    lower_pair(0, 2)
    ladder = climb_stages(0, 2)
    first_ladder = ladder
    side = lax.ppermute(ladder, "seq", flip_side)
    lower_pair(2, 3, jnp.minimum(jnp.abs(side[0, 0]), 0))
    gathered.append(with_other_core(jnp.concatenate([ladder, side], axis=0)))
    ladder = climb_stages(2, 4, first_ladder)
    done = attend(0, 0, 0, 2, (), ())
    ladder = wait_for(ladder, marks[0])
    side = lax.ppermute(ladder, "seq", flip_side)
    done = attend(1, 0, 0, 2, done, ())
    near = wait_for(jnp.concatenate([ladder, side], axis=0), marks[1])
    near = wait_for_moved(near, backs[0])
    gathered.append(with_other_core(near))
    lower_pair(3, 4, jnp.minimum(jnp.abs(near[0, 0]), 0))
    chip_a = reduce_chip(*done)
    done = attend(2, 1, 2, 3, (), (), 16)
    chip_a = wait_for(chip_a, marks[2])
    plane_a = reduce_plane(chip_a)
    chip_b = reduce_chip(*done)
    done = attend(3, 1, 3, 4, (), (backs[1], chip_a))
    chip_b = wait_for(chip_b, marks[3])
    plane_b = reduce_plane(chip_b)
    chip_c = wait_for_moved(reduce_chip(*done), backs[2])
    plane_c = reduce_plane(chip_c)
    group_a = reduce_group_halving(plane_a)
    merged = merge_call(wide_done[2], backs[:3], 0, ())
    plane_b = wait_for_moved(jnp.concatenate([plane_b, plane_c], axis=3), merged[0][None])
    group_b = wait_for_moved(reduce_group(plane_b), backs[3])
    merged = merge_call(wide_done[2], backs[3:], edges[3] * unit, tuple(merged))
    finished = place_call(rows_mine, reduce_half([group_a, group_b]), *merged)
    return (*wide_done[:2], *finished)


def solution(mesh):
    placed = (
        P(("seq", "head"), None),
        P(("seq", "head"), None),
        P(("seq", "head"), None),
        P(("seq", "head"), None),
        P("seq", None, None),
        P("seq", None),
    )
    paired = mesh.shape["head"] == 2 and mesh.shape["seq"] % 4 == 0
    return jax.shard_map(
        token_split if paired else per_device,
        mesh=mesh,
        in_specs=placed,
        out_specs=(
            P(("seq", "head"), None),
            P(("seq", "head"), None),
            P(("seq", "head"), None),
            P(("seq", "head"), None),
        ),
        check_vma=False,
    )
```
